512 devices in a mesh: site: 16 (over z), term: 32 (over y, x, core).
Axes of the slice: x: 4, y: 4, z: 16, core: 2. Of those that a mesh axis runs over, the one named last changes fastest.
Arguments:
- left_edge: float32 [128, 2, 128, 128], P('term'), as said below
- mps: float32 [64, 4, 2, 128, 128], P('site', None, None, None, 'term')
- block_list: int32 [64, 4, 2], P('site'), may hold values from 0 to 1, each once within a row
- coupling: float32 [128, 64, 4], P('term', 'site'), may hold values from 0.6 to 1.6
- right_env: float32 [16, 128, 2, 128, 128], P('site', 'term'), as said below
- start_vector: float32 [16, 2, 128, 128], P('site', None, None, 'term'), may hold values from -6 to 6
Outputs:
- env_out: float32 [16, 128, 2, 128, 128], P('site', 'term')
- state: float32 [16, 2, 128, 128], P('site', None, None, 'term')
- energy: float32 [16], P('site')
The draws below stay inside these ranges and needn't reach their ends.
Inputs may be any that keep to these rules, and one draw needn't show every extreme that they name: Each row of block_list names every one of the 2 sectors once. Every block of left_edge is symmetric. Every block of right_env is symmetric.
All inputs are finite; a program needn't handle non-finite values.
Results may differ from the reference program's by a relative error of at most 0.0003.
Values sent between devices are 32-bit elements; how exact they have to be, the bound alone decides.
A program may use at most 64 MiB of HBM per device.

```python
import math
import jax
import jax.numpy as jnp
from jax import lax

BLK = 128
SEC = 2
PHYS = 4
SITES_SEG = 4
ITERS = 4
SITES = 64
TERMS = 128
N_SITE = 16


def symmetric_noise(key, shape, scale):
    raw = jax.random.normal(key, shape, jnp.float32)
    return (raw + jnp.swapaxes(raw, -1, -2)) * (scale / jnp.sqrt(2.0 * BLK))


def draw_mps(key, part):
    key = jax.random.fold_in(key, 11)
    shape = (SITES, PHYS, SEC, BLK, BLK)
    noise = jax.random.normal(key, shape, jnp.float32) * (0.4 / jnp.sqrt(1.0 * BLK))
    identity = jnp.eye(BLK, dtype=jnp.float32)
    return (identity + noise) * (0.5 / jnp.sqrt(1.16))


def draw_left_edge(key, part):
    key = jax.random.fold_in(key, 23)
    first, second = jax.random.split(key)
    noise = symmetric_noise(first, (TERMS, SEC, BLK, BLK), 0.3)
    diagonal = jnp.exp(jax.random.uniform(second, (TERMS, SEC, BLK), jnp.float32, -0.693, 0.693))
    return noise + diagonal[..., None] * jnp.eye(BLK, dtype=jnp.float32)


def draw_right_env(key, part):
    key = jax.random.fold_in(key, 37)
    first, second, third, fourth = jax.random.split(key, 4)
    common = symmetric_noise(first, (N_SITE, 1, SEC, BLK, BLK), 0.3)
    own = symmetric_noise(second, (N_SITE, TERMS, SEC, BLK, BLK), 0.2)
    diagonal = jnp.exp(jax.random.uniform(third, (N_SITE, 1, SEC, BLK), jnp.float32, -0.693, 0.693))
    scales = jnp.exp(jax.random.uniform(fourth, (1, TERMS, 1, 1, 1), jnp.float32, -0.693, 0.693))
    return scales * (common + own + diagonal[..., None] * jnp.eye(BLK, dtype=jnp.float32))


def levels(key, shape, cuts, smallest, top_value):
    level = 1.0
    for position, parts in cuts:
        draws = jax.random.uniform(jax.random.fold_in(jax.random.fold_in(key, 6), position), (parts,), jnp.float32, smallest / len(cuts), top_value / len(cuts))
        level = level * jnp.repeat(jnp.exp(draws), shape[position] // parts).reshape((-1,) + (1,) * (len(shape) - 1 - position))
    return level


def gaussian(key, extent, width, limit, cuts=(), held_as=jnp.bfloat16):
    drawn = jax.random.normal(key, extent, jnp.float32) * width
    if len(cuts) > 0:
        drawn = levels(key, extent, cuts, -0.22, 0.18) * drawn
    return jnp.clip(drawn, min=-limit, max=limit).astype(held_as)


def setup_inputs(seed: int = 0) -> dict:
    seeds = jax.random.split(jax.random.key(seed), 7)
    return {
        "left_edge": draw_left_edge(jax.random.fold_in(seeds[6], 71), 0),
        "mps": draw_mps(jax.random.fold_in(seeds[6], 71), 0),
        "block_list": jax.vmap(lambda own: jax.random.permutation(own, SEC))(jax.random.split(seeds[2], SITES * PHYS)).reshape((SITES, PHYS, SEC)).astype(jnp.int32),
        "coupling": jnp.clip(jnp.exp(math.log(1.6) - 0.98082923 * jax.random.uniform(seeds[3], (TERMS, SITES, PHYS), jnp.float32) ** levels(seeds[3], (TERMS, SITES, PHYS), ((0, 32), (1, 16)), -0.2, 0.2)), 0.6, 1.6),
        "right_env": draw_right_env(jax.random.fold_in(seeds[6], 71), 0),
        "start_vector": gaussian(seeds[5], (N_SITE, SEC, BLK, BLK), 1.0, 6.0, ((0, 16), (3, 32)), jnp.float32),
    }


step_size = 0.5
epsilon = 1e-06

def env_step(environment, blocks, sector_map, weights):
    sectors = environment.shape[1]
    onehot = (sector_map[:, :, None] == jnp.arange(sectors, dtype=jnp.int32)[None, None, :]).astype(jnp.float32)
    sourced = jnp.einsum('pts,wsij->wptij', onehot, environment, precision=lax.Precision.HIGHEST)
    left_part = jnp.einsum('wptij,ptjk->wptik', sourced, blocks, precision=lax.Precision.HIGHEST)
    sandwich = jnp.einsum('ptji,wptjk->wptik', blocks, left_part, precision=lax.Precision.HIGHEST)
    return jnp.einsum('wp,wptik->wtik', weights, sandwich, precision=lax.Precision.HIGHEST)

def reference(left_edge, mps, block_list, coupling, right_env, start_vector):
    entries = SEC * BLK * BLK
    environment = left_edge
    leaving = []
    states = []
    energies = []
    for segment in range(N_SITE):
        entering = environment
        for within in range(SITES_SEG):
            orbital = segment * SITES_SEG + within
            environment = env_step(environment, mps[orbital], block_list[orbital], coupling[:, orbital, :])
        leaving.append(environment)
        right_side = right_env[segment]
        vector = start_vector[segment]
        vector = vector / jnp.sqrt(jnp.sum(vector * vector) / entries + epsilon)
        rayleigh = jnp.float32(0.0)
        for repeat in range(ITERS):
            product = jnp.einsum('wsij,sjk->wsik', entering, vector, precision=lax.Precision.HIGHEST)
            image = jnp.einsum('wsik,wskl->sil', product, right_side, precision=lax.Precision.HIGHEST) / TERMS
            rayleigh = jnp.sum(vector * image) / jnp.sum(vector * vector)
            corrected = vector - step_size * (image - rayleigh * vector)
            vector = corrected / jnp.sqrt(jnp.sum(corrected * corrected) / entries + epsilon)
        states.append(vector)
        energies.append(rayleigh)
    return (jnp.stack(leaving), jnp.stack(states), jnp.stack(energies).astype(jnp.float32))
```

```python
import functools

import jax
import jax.numpy as jnp
from jax import lax
from jax.experimental import pallas as pl
from jax.experimental.pallas import tpu as pltpu
from jax.sharding import PartitionSpec as P

ITERS = 4
STEP = 0.5
EPSILON = 1e-06
N = 128
ORB = 4
PHYS = 4
SEC = 2
WORK = 4
MESH = pl.DeviceIdType.MESH
F32, BF16 = jnp.float32, jnp.bfloat16


def split(x):
    high = x.astype(BF16)
    return high, (x - high.astype(F32)).astype(BF16)


def dot(a, b):
    return lax.dot_general(a, b, (((1,), (0,)), ((), ())), preferred_element_type=F32)


def kernel(
    sites,
    terms,
    perm_ref,
    coup_ref,
    left_ref,
    mps_ref,
    right_ref,
    start_ref,
    env_ref,
    state_ref,
    energy_ref,
    mine,
    theirs,
    slab,
    full,
    starts,
    weights_b,
    weights_t,
    enter,
    enter_hl,
    right_hl,
    cur,
    tx,
    rx,
    vec,
    part,
    pieces,
    reduced,
    gathered,
    pair_ss,
    pair_rs,
    orb_ss,
    orb_rs,
    fwd_ss,
    fwd_rs,
    vec_ss,
    vec_rs,
    tx_sem,
    rx_sem,
    red_ss,
    red_rs,
    gat_ss,
    gat_rs,
):
    site = lax.axis_index("site")
    me = lax.axis_index("term")
    chip, core = me // 2, me % 2
    chips = terms // 2
    sibling = chip * 2 + (1 - core)
    last = sites - 1

    barrier = pltpu.get_barrier_semaphore()

    def greet(d, carry):
        pl.semaphore_signal(barrier, inc=1, device_id={"term": lax.rem(me + d, terms)}, device_id_type=MESH)
        return carry

    lax.fori_loop(1, terms, greet, 0)

    @pl.when(site > 0)
    def _():
        pl.semaphore_signal(barrier, inc=1, device_id={"site": site - 1}, device_id_type=MESH)

    @pl.when(site < last)
    def _():
        pl.semaphore_signal(barrier, inc=1, device_id={"site": site + 1}, device_id_type=MESH)

    shard = mps_ref[...]
    mine[0 : ORB * 8] = jnp.concatenate([shard, shard], axis=1)
    own = start_ref[...]
    mine[ORB * 8 : ORB * 8 + SEC] = jnp.concatenate([own, own], axis=1)
    greeted = terms - 1 + jnp.where(site > 0, 1, 0) + jnp.where(site < last, 1, 0)
    pl.semaphore_wait(barrier, greeted)

    pair = pltpu.make_async_remote_copy(
        src_ref=mine, dst_ref=theirs, send_sem=pair_ss, recv_sem=pair_rs,
        device_id={"term": sibling}, device_id_type=MESH,
    )
    pair.start()
    pair.wait()
    half = lax.broadcasted_iota(jnp.int32, (ORB * 8 + SEC, 8, N), 1) // 4
    slab[...] = jnp.where(half == core, mine[...], theirs[...])

    def spread(o, carry):
        source = slab.at[pl.ds(o * 8 + core * 4, 4)]
        pltpu.make_async_copy(source, full.at[o, chip, core], orb_rs.at[o]).start()

        def peer_copy(d, c):
            peer = lax.rem(chip + d, chips) * 2 + core
            pltpu.make_async_remote_copy(
                src_ref=source, dst_ref=full.at[o, chip, core], send_sem=orb_ss.at[o], recv_sem=orb_rs.at[o],
                device_id={"term": peer}, device_id_type=MESH,
            ).start()
            return c

        lax.fori_loop(1, chips, peer_copy, 0)
        return carry

    lax.fori_loop(0, ORB, spread, 0)
    vec_source = slab.at[pl.ds(ORB * 8, SEC)]
    pltpu.make_async_copy(vec_source, starts.at[chip], vec_rs).start()

    def vec_copy(d, c):
        peer = lax.rem(chip + d, chips) * 2 + core
        pltpu.make_async_remote_copy(
            src_ref=vec_source, dst_ref=starts.at[chip], send_sem=vec_ss, recv_sem=vec_rs,
            device_id={"term": peer}, device_id_type=MESH,
        ).start()
        return c

    lax.fori_loop(1, chips, vec_copy, 0)

    def prepare_right(w, carry):
        for s in range(SEC):
            high, low = split(right_ref[w, s])
            right_hl[s, pl.ds(w * N, N), 0:N] = high
            right_hl[s, pl.ds(w * N, N), N : 2 * N] = low
        return carry

    lax.fori_loop(0, WORK, prepare_right, 0)

    def forward(o):
        return pltpu.make_async_remote_copy(
            src_ref=full.at[o, :, core], dst_ref=full.at[o, :, core], send_sem=fwd_ss.at[o], recv_sem=fwd_rs.at[o],
            device_id={"term": sibling}, device_id_type=MESH,
        )

    def prepare(o):
        pltpu.make_async_copy(full.at[o, :, core], full.at[o, :, core], orb_rs.at[o]).wait()
        forward(o).start()
        pltpu.make_async_copy(full.at[o, :, 1 - core], full.at[o, :, 1 - core], fwd_rs.at[o]).wait()
        for p in range(PHYS):
            blocks = [full[o, :, p // 2, (p % 2) * SEC + t].reshape(N, N) for t in range(SEC)]
            columns = slice(p * N, (p + 1) * N)
            for t in range(SEC):
                high, low = split(blocks[t])
                weights_t[o, t, 0, :, columns] = high * BF16(0.5)
                weights_t[o, t, 1, :, columns] = low
            first = perm_ref[(o * PHYS + p) * SEC]
            for s in range(SEC):
                block = jnp.where(first == s, blocks[0], blocks[1]).T.astype(BF16)
                weights_b[o, s, 0:N, columns] = block
                weights_b[o, s, N : 2 * N, columns] = block

    def orbital(w, o):
        moved = []
        for s in range(SEC):
            high, low = split(cur[s])
            moved.append(dot(jnp.concatenate([high, low], axis=1), weights_b[o, s]))
        for t in range(SEC):
            highs, lows = [], []
            for p in range(PHYS):
                columns = slice(p * N, (p + 1) * N)
                source = perm_ref[(o * PHYS + p) * SEC + t]
                weight = coup_ref[(w * ORB + o) * PHYS + p]
                high, low = split(jnp.where(source == 0, moved[0][:, columns], moved[1][:, columns]) * weight)
                highs.append(high)
                lows.append(low)
            high, low = jnp.concatenate(highs, axis=0), jnp.concatenate(lows, axis=0)
            wide = dot(weights_t[o, t, 0], jnp.concatenate([high, low], axis=1))
            y = wide[:, :N] + wide[:, N:] + dot(weights_t[o, t, 1], high)
            cur[t] = y + y.T

    row = lax.broadcasted_iota(jnp.int32, (N, N), 0)
    column = lax.broadcasted_iota(jnp.int32, (N, N), 1)

    def advance(w, first):
        cur[...] = enter[w]

        def one(o, carry):
            if first is not None:
                pl.when(first)(lambda: prepare(o))
            orbital(w, o)
            return carry

        lax.fori_loop(0, ORB, one, 0)
        env_ref[w] = cur[...]

    def chain_copy(w):
        return pltpu.make_async_remote_copy(
            src_ref=tx.at[w], dst_ref=rx.at[w], send_sem=tx_sem.at[w], recv_sem=rx_sem.at[w],
            device_id={"site": lax.rem(site + 1, sites)}, device_id_type=MESH,
        )

    @pl.when(site > 0)
    def _():
        def early(o, carry):
            prepare(o)
            return carry

        lax.fori_loop(0, ORB, early, 0)

    def chain(w, carry):
        @pl.when(site == 0)
        def _():
            enter[w] = left_ref[w]

        @pl.when(site > 0)
        def _():
            chain_copy(w).wait_recv()
            packed = rx[w, 0:N]
            flipped = packed.T
            diagonal = rx[w, N : N + 1]
            enter[w, 0] = jnp.where(row <= column, packed, flipped)
            enter[w, 1] = jnp.where(row > column, packed, jnp.where(row < column, flipped, diagonal))

        @pl.when(site < last)
        def _():
            advance(w, jnp.logical_and(site == 0, w == 0))
            tx[w, 0:N] = jnp.where(row <= column, cur[0], cur[1])
            diagonal = jnp.sum(jnp.where(row == column, cur[1], 0.0), axis=0, keepdims=True)
            tx[w, N : N + 8] = jnp.broadcast_to(diagonal, (8, N))
            chain_copy(w).start()

        for s in range(SEC):
            high, low = split(enter[w, s])
            enter_hl[s, pl.ds(w * N, N), 0:N] = high
            enter_hl[s, pl.ds(w * N, N), N : 2 * N] = low
        return carry

    lax.fori_loop(0, WORK, chain, 0)

    entries = SEC * N * N
    pltpu.make_async_copy(starts, starts, vec_rs).wait()
    u = [starts[:, s].reshape(N, N) for s in range(SEC)]
    scale = jnp.sqrt((jnp.sum(u[0] * u[0]) + jnp.sum(u[1] * u[1])) / entries + EPSILON)
    for s in range(SEC):
        vec[s] = u[s] / scale

    def iteration(it, carry):
        slot = lax.rem(it, 2)
        for s in range(SEC):
            high, low = split(vec[s])
            sides = jnp.concatenate(
                [jnp.concatenate([high, low], axis=1), jnp.concatenate([high, jnp.zeros_like(high)], axis=1)], axis=0
            )
            wide = dot(right_hl[s], sides)
            product = wide[:, :N] + wide[:, N:]
            high, low = split(product)
            high = jnp.concatenate([high[w * N : (w + 1) * N] for w in range(WORK)], axis=1)
            low = jnp.concatenate([low[w * N : (w + 1) * N] for w in range(WORK)], axis=1)
            wide = dot(high, enter_hl[s])
            total = wide[:, :N] + wide[:, N:] + dot(low, enter_hl[s, :, 0:N])
            part[slot, pl.ds(s * (N // 8), N // 8)] = total.reshape(N // 8, 8, N)

        pltpu.make_async_copy(part.at[slot, me], pieces.at[slot, me], red_rs.at[slot]).start()

        def scatter(d, c):
            peer = lax.rem(me + d, terms)
            pltpu.make_async_remote_copy(
                src_ref=part.at[slot, peer], dst_ref=pieces.at[slot, me], send_sem=red_ss.at[slot],
                recv_sem=red_rs.at[slot], device_id={"term": peer}, device_id_type=MESH,
            ).start()
            return c

        lax.fori_loop(1, terms, scatter, 0)

        @pl.when(site == last)
        def _():
            advance(it, None)

        pltpu.make_async_copy(pieces.at[slot], pieces.at[slot], red_rs.at[slot]).wait()
        reduced[slot] = jnp.sum(pieces[slot], axis=0) * (1.0 / (WORK * terms))
        pltpu.make_async_copy(reduced.at[slot], gathered.at[slot, me], gat_rs.at[slot]).start()

        def share(d, c):
            peer = lax.rem(me + d, terms)
            pltpu.make_async_remote_copy(
                src_ref=reduced.at[slot], dst_ref=gathered.at[slot, me], send_sem=gat_ss.at[slot],
                recv_sem=gat_rs.at[slot], device_id={"term": peer}, device_id_type=MESH,
            ).start()
            return c

        lax.fori_loop(1, terms, share, 0)
        pltpu.make_async_copy(gathered.at[slot], gathered.at[slot], gat_rs.at[slot]).wait()
        sent = pieces.at[slot, pl.ds(0, terms - 1)]
        pltpu.make_async_copy(sent, sent, red_ss.at[slot]).wait()
        pltpu.make_async_copy(sent, sent, gat_ss.at[slot]).wait()

        image = gathered[slot].reshape(SEC, N, N)
        old = vec[...]
        rayleigh = jnp.sum(old * image) / jnp.sum(old * old)
        corrected = old - STEP * (image - rayleigh * old)
        vec[...] = corrected / jnp.sqrt(jnp.sum(corrected * corrected) / entries + EPSILON)
        energy_ref[0, 0] = rayleigh
        return carry

    lax.fori_loop(0, ITERS, iteration, 0)
    for s in range(SEC):
        rows = vec[s, pl.ds(pl.multiple_of(chip * 8, 8), 8)]
        state_ref[s] = jnp.where(core == 0, rows[0:4], rows[4:8])

    def spread_done(o, carry):
        part_sent = full.at[o, pl.ds(0, chips - 1), 0]
        pltpu.make_async_copy(part_sent, part_sent, orb_ss.at[o]).wait()
        forward(o).wait_send()
        return carry

    lax.fori_loop(0, ORB, spread_done, 0)
    vec_sent = starts.at[pl.ds(0, chips - 1)]
    pltpu.make_async_copy(vec_sent, vec_sent, vec_ss).wait()

    @pl.when(site < last)
    def _():
        def chain_done(w, carry):
            chain_copy(w).wait_send()
            return carry

        lax.fori_loop(0, WORK, chain_done, 0)


def solution(mesh):
    sites, terms = mesh.shape["site"], mesh.shape["term"]
    chips = terms // 2

    def body(left_edge, mps, block_list, coupling, right_env, start_vector):
        shard = jnp.swapaxes(mps, 3, 4).reshape(ORB * 8, 4, N)
        start = jnp.swapaxes(start_vector[0], 1, 2)
        vmem = pl.BlockSpec(memory_space=pltpu.VMEM)
        smem = pl.BlockSpec(memory_space=pltpu.SMEM)
        dma = pltpu.SemaphoreType.DMA
        env, state, energy = pl.pallas_call(
            functools.partial(kernel, sites, terms),
            out_shape=(
                jax.ShapeDtypeStruct((WORK, SEC, N, N), F32),
                jax.ShapeDtypeStruct((SEC, 4, N), F32),
                jax.ShapeDtypeStruct((1, 1), F32),
            ),
            in_specs=[smem, smem, vmem, vmem, vmem, vmem],
            out_specs=(vmem, vmem, smem),
            scratch_shapes=[
                pltpu.VMEM((ORB * 8 + SEC, 8, N), F32),
                pltpu.VMEM((ORB * 8 + SEC, 8, N), F32),
                pltpu.VMEM((ORB * 8 + SEC, 8, N), F32),
                pltpu.VMEM((ORB, chips, 2, 4, 8, N), F32),
                pltpu.VMEM((chips, SEC, 8, N), F32),
                pltpu.VMEM((ORB, SEC, 2 * N, PHYS * N), BF16),
                pltpu.VMEM((ORB, SEC, 2, N, PHYS * N), BF16),
                pltpu.VMEM((WORK, SEC, N, N), F32),
                pltpu.VMEM((SEC, WORK * N, 2 * N), BF16),
                pltpu.VMEM((SEC, WORK * N, 2 * N), BF16),
                pltpu.VMEM((SEC, N, N), F32),
                pltpu.VMEM((WORK, N + 8, N), F32),
                pltpu.VMEM((WORK, N + 8, N), F32),
                pltpu.VMEM((SEC, N, N), F32),
                pltpu.VMEM((2, terms, 8, N), F32),
                pltpu.VMEM((2, terms, 8, N), F32),
                pltpu.VMEM((2, 8, N), F32),
                pltpu.VMEM((2, terms, 8, N), F32),
                dma, dma, dma((ORB,)), dma((ORB,)), dma((ORB,)), dma((ORB,)), dma, dma,
                dma((WORK,)), dma((WORK,)), dma((2,)), dma((2,)), dma((2,)), dma((2,)),
            ],
            compiler_params=pltpu.CompilerParams(
                collective_id=0, has_side_effects=True, vmem_limit_bytes=40 * 1024 * 1024
            ),
        )(block_list.reshape(-1), coupling.reshape(-1), left_edge, shard, right_env[0], start)
        return env[None], jnp.swapaxes(state, 1, 2)[None], energy.reshape(1)

    in_specs = (
        P("term", None, None, None),
        P("site", None, None, None, "term"),
        P("site", None, None),
        P("term", "site", None),
        P("site", "term", None, None, None),
        P("site", None, None, "term"),
    )
    out_specs = (P("site", "term", None, None, None), P("site", None, None, "term"), P("site"))
    return jax.shard_map(body, mesh=mesh, in_specs=in_specs, out_specs=out_specs, check_vma=False)
```

```python
import functools

import jax
import jax.numpy as jnp
from jax import lax
from jax.experimental import pallas as pl
from jax.experimental.pallas import tpu as pltpu
from jax.sharding import PartitionSpec as P

ITERS = 4
STEP = 0.5
EPSILON = 1e-06
N = 128
ORB = 4
PHYS = 4
SEC = 2
WORK = 4
PLANES = 4
GROUPS = ((0, 2, 0, 3), (2, 3, 2, 5), (5, 5, 3, 6), (10, 6, 5, 9))
DEEP = max(group[1] for group in GROUPS)
SIDE = 4
MESH = pl.DeviceIdType.MESH
F32, BF16 = jnp.float32, jnp.bfloat16


def split(x):
    high = x.astype(BF16)
    return high, (x - high.astype(F32)).astype(BF16)


def dot(a, b):
    return lax.dot_general(a, b, (((1,), (0,)), ((), ())), preferred_element_type=F32)


def by_plane(plane, field):
    value = jnp.int32(GROUPS[0][field])
    for index, group in enumerate(GROUPS):
        value = jnp.where(plane >= index * PLANES, group[field], value)
    return value


def first_plane(segment):
    value = jnp.int32(0)
    for index, group in enumerate(GROUPS):
        value = jnp.where(segment >= group[0], index * PLANES, value)
    return value


def greetings(sites):
    carrier = {}
    for index, (first, depth, _, _) in enumerate(GROUPS):
        for segment in range(first, first + depth):
            carrier[segment] = index * PLANES
    early, late = set(), set()
    for segment, base in carrier.items():
        early |= {(segment, base + r) for r in range(PLANES)}
        for r in range(PLANES):
            late.add((base + r, segment))
            if segment + 1 < sites:
                late |= {(base + r, carrier[segment + 1] + r), (base + r, segment + 1)}
    early = {(a, b) for a, b in early if a != b}
    late = {(a, b) for a, b in late if a != b and (a, b) not in early}
    return {(b, a) for a, b in early} | late, {(b, a) for a, b in late}


def lookup(site, values):
    chosen = jnp.int32(0)
    for plane, value in enumerate(values):
        chosen = jnp.where(site == plane, value, chosen)
    return chosen


def kernel(
    sites,
    terms,
    perm_ref,
    coup_ref,
    left_ref,
    mps_ref,
    right_ref,
    start_ref,
    env_ref,
    state_ref,
    energy_ref,
    left_in,
    mps_in,
    right_in,
    start_in,
    mine,
    theirs,
    slab,
    slabs,
    coef,
    lanes,
    coefs,
    full,
    starts,
    weights_b,
    weights_t,
    enter_hl,
    right_hl,
    cur,
    tx,
    rx,
    vec,
    part,
    pieces,
    reduced,
    gathered,
    pair_ss,
    pair_rs,
    slab_ss,
    slab_rs,
    coef_ss,
    coef_rs,
    leg_ss,
    leg_rs,
    orb_ss,
    orb_rs,
    fwd_ss,
    fwd_rs,
    vec_ss,
    vec_rs,
    tx_sem,
    rx_sem,
    red_ss,
    red_rs,
    gat_ss,
    gat_rs,
    load_sem,
    answered,
):
    site = lax.axis_index("site")
    me = lax.axis_index("term")
    chip, core = me // 2, me % 2
    chips = terms // 2
    sibling = chip * 2 + (1 - core)
    last = sites - 1
    first, depth, ready, steps = (by_plane(site, field) for field in range(4))
    term = lax.rem(site, PLANES)
    x, y = chip % SIDE, chip // SIDE

    loads = [
        pltpu.make_async_copy(outside, inside, load_sem.at[index])
        for index, (outside, inside) in enumerate(
            ((mps_ref, mps_in), (start_ref, start_in), (left_ref, left_in), (right_ref, right_in))
        )
    ]
    for load in loads:
        load.start()

    def along_x(d):
        return {"term": (y * SIDE + lax.rem(x + d, SIDE)) * 2 + core}

    def along_y(d):
        return {"term": (lax.rem(y + d, SIDE) * SIDE + x) * 2 + core}

    barrier = pltpu.get_barrier_semaphore()
    for d in range(1, SIDE):
        for line in (along_x, along_y):
            pl.semaphore_signal(barrier, inc=1, device_id=line(d), device_id_type=MESH)
    pl.semaphore_signal(barrier, inc=1, device_id={"term": sibling}, device_id_type=MESH)
    entry, answers = greetings(sites)

    def signal_planes(pairs, semaphore):
        mask = lookup(site, [sum(1 << b for a, b in pairs if a == plane) for plane in range(sites)])

        def one(other, carry):
            @pl.when((mask >> other) % 2 == 1)
            def _():
                pl.semaphore_signal(semaphore, inc=1, device_id={"site": other}, device_id_type=MESH)

            return carry

        lax.fori_loop(0, sites, one, 0)

    def greeted(pairs):
        return lookup(site, [sum(1 for a, b in pairs if b == plane) for plane in range(sites)])

    signal_planes(entry, barrier)

    loads[0].wait()
    loads[1].wait()
    shard = mps_in[...]
    shard = jnp.concatenate([shard, shard], axis=1).reshape(ORB, 2, 4, 8, N)
    for h in range(2):
        mine[h * 16 : (h + 1) * 16] = shard[:, h].reshape(16, 8, N)
    own = start_in[...]
    mine[32 : 32 + SEC] = jnp.concatenate([own, own], axis=1)

    lane = lax.broadcasted_iota(jnp.int32, (8, N), 1)

    compact = jnp.zeros((8, N), F32)
    for w in range(WORK):
        for o in range(ORB):
            for p in range(PHYS):
                compact = jnp.where(lane == (w * ORB + o) * PHYS + p, coup_ref[w, o, p], compact)
    for o in range(ORB):
        for p in range(PHYS):
            for t in range(SEC):
                index = WORK * ORB * PHYS + (o * PHYS + p) * SEC + t
                compact = jnp.where(lane == index, perm_ref[o, p, t].astype(F32), compact)
    coef[...] = compact
    pl.semaphore_wait(barrier, 2 * (SIDE - 1) + 1 + greeted(entry))
    signal_planes(answers, answered)

    pair = pltpu.make_async_remote_copy(
        src_ref=mine, dst_ref=theirs, send_sem=pair_ss, recv_sem=pair_rs,
        device_id={"term": sibling}, device_id_type=MESH,
    )
    pair.start()
    pair.wait()
    half = lax.broadcasted_iota(jnp.int32, (32 + SEC, 8, N), 1) // 4
    slab[...] = jnp.where(half == core, mine[...], theirs[...])

    source = slab.at[pl.ds(core * 16, 16)]
    to_base = first_plane(site)

    place_of = site - by_plane(to_base, 0)

    def slab_copies(r):
        return [
            pltpu.make_async_remote_copy(
                src_ref=src, dst_ref=dst, send_sem=ss.at[r], recv_sem=rs.at[place_of],
                device_id={"site": to_base + r}, device_id_type=MESH,
            )
            for src, dst, ss, rs in (
                (source, slabs.at[place_of], slab_ss, slab_rs),
                (coef, lanes.at[place_of], coef_ss, coef_rs),
            )
        ]

    def slab_send(r, carry):
        @pl.when(to_base + r == site)
        def _():
            pltpu.make_async_copy(source, slabs.at[place_of], slab_rs.at[place_of]).start()
            pltpu.make_async_copy(coef, lanes.at[place_of], coef_rs.at[place_of]).start()

        @pl.when(to_base + r != site)
        def _():
            for copy in slab_copies(r):
                copy.start()

        return carry

    lax.fori_loop(0, PLANES, slab_send, 0)

    def tiles_of(o):
        return pl.ds(o * 4, 4)

    def row_of(q, o, r):
        return full.at[q, r, :, core, tiles_of(o)]

    def column_of(q, o, c):
        return full.at[q, :, c, core, tiles_of(o)]

    def first_leg(q, o):
        place = full.at[q, y, x, core, tiles_of(o)]
        tiles = slabs.at[q, tiles_of(o)]
        pltpu.make_async_copy(tiles, place, leg_rs.at[q, o]).start()
        for d in range(1, SIDE):
            pltpu.make_async_remote_copy(
                src_ref=tiles, dst_ref=place, send_sem=leg_ss.at[q], recv_sem=leg_rs.at[q, o],
                device_id=(along_x, along_y)[o % 2](d), device_id_type=MESH,
            ).start()

    def second_leg(q, o):
        line = row_of(q, o, y) if o % 2 == 0 else column_of(q, o, x)
        pltpu.make_async_copy(line, line, leg_rs.at[q, o]).wait()
        for d in range(1, SIDE):
            pltpu.make_async_remote_copy(
                src_ref=line, dst_ref=line, send_sem=orb_ss.at[q], recv_sem=orb_rs.at[q, o, d - 1],
                device_id=(along_y, along_x)[o % 2](d), device_id_type=MESH,
            ).start()

    def arrived(q, o, parity):
        for d in range(1, SIDE):
            if parity == 0:
                line = row_of(q, o, lax.rem(y + SIDE - d, SIDE))
            else:
                line = column_of(q, o, lax.rem(x + SIDE - d, SIDE))
            pltpu.make_async_copy(line, line, orb_rs.at[q, o, d - 1]).wait()

    def forward(q, o):
        tiles = full.at[q, :, :, core, tiles_of(o)]
        return pltpu.make_async_remote_copy(
            src_ref=tiles, dst_ref=tiles, send_sem=fwd_ss.at[q, o], recv_sem=fwd_rs.at[q, o],
            device_id={"term": sibling}, device_id_type=MESH,
        )

    def gather_step(i):
        @pl.when(i < depth)
        def _():
            pltpu.make_async_copy(slabs.at[i], slabs.at[i], slab_rs.at[i]).wait()
            pltpu.make_async_copy(lanes.at[i], lanes.at[i], coef_rs.at[i]).wait()
            for o in range(ORB):
                first_leg(i, o)
            coefs[i] = jnp.broadcast_to(lanes[i, 0:1], (N, N)).T

        @pl.when(jnp.logical_and(i >= 1, i < depth + 1))
        def _():
            for o in range(ORB):
                second_leg(i - 1, o)

        @pl.when(jnp.logical_and(i >= 3, i < depth + 3))
        def _():
            for o in range(ORB):
                arrived(i - 3, o, o % 2)
                forward(i - 3, o).start()

    def gather_loop(i, carry):
        gather_step(i)
        return carry

    lax.fori_loop(0, steps, gather_loop, 0)

    vec_source = slab.at[pl.ds(32, SEC)]

    def side_work():
        pltpu.make_async_copy(vec_source, starts.at[chip], vec_rs).start()

        def vec_copy(d, c):
            peer = lax.rem(chip + d, chips) * 2 + core
            pltpu.make_async_remote_copy(
                src_ref=vec_source, dst_ref=starts.at[chip], send_sem=vec_ss, recv_sem=vec_rs,
                device_id={"term": peer}, device_id_type=MESH,
            ).start()
            return c

        lax.fori_loop(1, chips, vec_copy, 0)

        loads[3].wait()

        def prepare_right(w, carry):
            for s in range(SEC):
                high, low = split(right_in[w, s])
                right_hl[s, pl.ds(w * N, N), 0:N] = high
                right_hl[s, pl.ds(w * N, N), N : 2 * N] = low
            return carry

        lax.fori_loop(0, WORK, prepare_right, 0)

    pl.when(ready > 0)(side_work)

    def coefficient(q, index):
        return coefs[q, pl.ds(index, 1)]

    def sector(q, o, p, t):
        return coefficient(q, WORK * ORB * PHYS + (o * PHYS + p) * SEC + t)

    def prepare(q, o):
        there = full.at[q, :, :, 1 - core, tiles_of(o)]
        pltpu.make_async_copy(there, there, fwd_rs.at[q, o]).wait()
        for p in range(PHYS):
            blocks = [full[q, :, :, p // 2, o * 4 + (p % 2) * SEC + t].reshape(N, N) for t in range(SEC)]
            columns = slice(p * N, (p + 1) * N)
            for t in range(SEC):
                high, low = split(blocks[t])
                weights_t[q, o, t, 0, :, columns] = high * BF16(0.5)
                weights_t[q, o, t, 1, :, columns] = low
            source_of_first = sector(q, o, p, 0)
            for s in range(SEC):
                weights_b[q, o, s, :, columns] = jnp.where(source_of_first == s, blocks[0], blocks[1]).T.astype(BF16)

    def orbital(q, o):
        moved = []
        for s in range(SEC):
            high, low = split(cur[s])
            block = weights_b[q, o, s]
            moved.append(dot(jnp.concatenate([high, low], axis=1), jnp.concatenate([block, block], axis=0)))
        for t in range(SEC):
            highs, lows = [], []
            for p in range(PHYS):
                columns = slice(p * N, (p + 1) * N)
                source_sector = sector(q, o, p, t)
                weight = coefficient(q, (term * ORB + o) * PHYS + p)
                high, low = split(jnp.where(source_sector == 0, moved[0][:, columns], moved[1][:, columns]) * weight)
                highs.append(high)
                lows.append(low)
            high, low = jnp.concatenate(highs, axis=0), jnp.concatenate(lows, axis=0)
            wide = dot(weights_t[q, o, t, 0], jnp.concatenate([high, low], axis=1))
            y = wide[:, :N] + wide[:, N:] + dot(weights_t[q, o, t, 1], high)
            cur[t] = y + y.T

    row = lax.broadcasted_iota(jnp.int32, (N, N), 0)
    column = lax.broadcasted_iota(jnp.int32, (N, N), 1)

    def unpack(kind, w):
        packed = rx[kind, w, 0:N]
        flipped = packed.T
        diagonal = rx[kind, w, N : N + 1]
        return (
            jnp.where(row <= column, packed, flipped),
            jnp.where(row > column, packed, jnp.where(row < column, flipped, diagonal)),
        )

    def message(kind, w, slot, plane):
        return pltpu.make_async_remote_copy(
            src_ref=tx.at[slot], dst_ref=rx.at[kind, w], send_sem=tx_sem.at[kind, slot], recv_sem=rx_sem.at[kind, w],
            device_id={"site": plane}, device_id_type=MESH,
        )

    def received(kind, w):
        pltpu.make_async_copy(rx.at[kind, w], rx.at[kind, w], rx_sem.at[kind, w]).wait()

    def act(copy, start):
        if start:
            copy.start()
        else:
            copy.wait_send()

    def messages(q, start):
        segment = first + q
        after = lax.rem(segment + 1, sites)
        goes_on = jnp.logical_and(q == depth - 1, segment < last)
        pl.when(goes_on)(lambda: act(message(0, term, q, first_plane(after) + term), start))
        pl.when(jnp.logical_and(segment < last, after != site))(lambda: act(message(1, term, q, after), start))
        if start:

            @pl.when(jnp.logical_and(segment < last, after == site))
            def _():
                pltpu.make_async_copy(tx.at[q], rx.at[1, term], rx_sem.at[1, term]).start()

    def results(q, start):
        pl.when(first + q != site)(lambda: act(message(2, term, q, first + q), start))

    def early(index, carry):
        prepare(index // ORB, index % ORB)
        return carry

    lax.fori_loop(0, ready * ORB, early, 0)
    loads[2].wait()
    pl.semaphore_wait(answered, greeted(answers))

    @pl.when(first == 0)
    def _():
        cur[...] = left_in[term]

    @pl.when(first > 0)
    def _():
        received(0, term)
        cur[0], cur[1] = unpack(0, term)

    def one_segment(q, c):
        pl.when(q + 3 >= steps)(lambda: gather_step(q + 3))

        def one(o, cc):
            pl.when(q >= ready)(lambda: prepare(q, o))
            orbital(q, o)
            return cc

        lax.fori_loop(0, ORB, one, 0)
        tx[q, 0:N] = jnp.where(row <= column, cur[0], cur[1])
        diagonal = jnp.sum(jnp.where(row == column, cur[1], 0.0), axis=0, keepdims=True)
        tx[q, N : N + 8] = jnp.broadcast_to(diagonal, (8, N))
        messages(q, True)

        @pl.when(first + q == site)
        def _():
            env_ref[term] = cur[...]

        return c

    lax.fori_loop(0, depth, one_segment, 0)

    def results_start(q, carry):
        results(q, True)
        return carry

    lax.fori_loop(0, depth, results_start, 0)
    pl.when(ready == 0)(side_work)

    def entering(w, carry):
        pl.when(site > 0)(lambda: received(1, w))

        def keep(blocks):
            for s in range(SEC):
                high, low = split(blocks[s])
                enter_hl[s, pl.ds(w * N, N), 0:N] = high
                enter_hl[s, pl.ds(w * N, N), N : 2 * N] = low

        pl.when(site == 0)(lambda: keep((left_in[w, 0], left_in[w, 1])))
        pl.when(site > 0)(lambda: keep(unpack(1, w)))
        return carry

    lax.fori_loop(0, WORK, entering, 0)

    entries = SEC * N * N
    pltpu.make_async_copy(starts, starts, vec_rs).wait()
    u = [starts[:, s].reshape(N, N) for s in range(SEC)]
    scale = jnp.sqrt((jnp.sum(u[0] * u[0]) + jnp.sum(u[1] * u[1])) / entries + EPSILON)
    for s in range(SEC):
        vec[s] = u[s] / scale

    def total_of(values):
        return jnp.sum(values, axis=(0, 1, 2), keepdims=True)

    offsets = sorted(
        ((a, b, c) for a in range(SIDE) for b in range(SIDE) for c in range(2) if (a, b, c) != (0, 0, 0)),
        key=lambda abc: -min(abc[0], SIDE - abc[0]) - min(abc[1], SIDE - abc[1]),
    )
    far_first = [
        (lax.rem(y + a, SIDE) * SIDE + lax.rem(x + b, SIDE)) * 2 + (core if c == 0 else 1 - core) for a, b, c in offsets
    ]

    def iteration(it, carry):
        slot = lax.rem(it, 2)
        for s in range(SEC):
            high, low = split(vec[s])
            sides = jnp.concatenate(
                [jnp.concatenate([high, low], axis=1), jnp.concatenate([high, jnp.zeros_like(high)], axis=1)], axis=0
            )
            wide = dot(right_hl[s], sides)
            product = wide[:, :N] + wide[:, N:]
            high, low = split(product)
            high = jnp.concatenate([high[w * N : (w + 1) * N] for w in range(WORK)], axis=1)
            low = jnp.concatenate([low[w * N : (w + 1) * N] for w in range(WORK)], axis=1)
            wide = dot(high, enter_hl[s])
            total = wide[:, :N] + wide[:, N:] + dot(low, enter_hl[s, :, 0:N])
            part[slot, pl.ds(s * (N // 8), N // 8)] = total.reshape(N // 8, 8, N)

        pltpu.make_async_copy(part.at[slot, me], pieces.at[slot, me], red_rs.at[slot]).start()

        for peer in far_first:
            pltpu.make_async_remote_copy(
                src_ref=part.at[slot, peer], dst_ref=pieces.at[slot, me], send_sem=red_ss.at[slot],
                recv_sem=red_rs.at[slot], device_id={"term": peer}, device_id_type=MESH,
            ).start()

        old = vec[...]
        square = total_of(old * old)

        pltpu.make_async_copy(pieces.at[slot], pieces.at[slot], red_rs.at[slot]).wait()
        reduced[slot] = jnp.sum(pieces[slot], axis=0) * (1.0 / (WORK * terms))
        pltpu.make_async_copy(reduced.at[slot], gathered.at[slot, me], gat_rs.at[slot]).start()

        for peer in far_first:
            pltpu.make_async_remote_copy(
                src_ref=reduced.at[slot], dst_ref=gathered.at[slot, me], send_sem=gat_ss.at[slot],
                recv_sem=gat_rs.at[slot], device_id={"term": peer}, device_id_type=MESH,
            ).start()

        pltpu.make_async_copy(gathered.at[slot], gathered.at[slot], gat_rs.at[slot]).wait()
        sent = pieces.at[slot, pl.ds(0, terms - 1)]
        pltpu.make_async_copy(sent, sent, red_ss.at[slot]).wait()
        pltpu.make_async_copy(sent, sent, gat_ss.at[slot]).wait()

        image = gathered[slot].reshape(SEC, N, N)
        rayleigh = total_of(old * image) / square
        corrected = old - STEP * (image - rayleigh * old)
        vec[...] = corrected / jnp.sqrt(total_of(corrected * corrected) / entries + EPSILON)
        energy_ref[...] = jnp.broadcast_to(rayleigh[0], (8, N))
        return carry

    lax.fori_loop(0, ITERS, iteration, 0)
    for s in range(SEC):
        rows = vec[s, pl.ds(pl.multiple_of(chip * 8, 8), 8)]
        state_ref[s] = jnp.where(core == 0, rows[0:4], rows[4:8])

    def leaving(w, carry):
        @pl.when(first_plane(site) + w != site)
        def _():
            received(2, w)
            env_ref[w, 0], env_ref[w, 1] = unpack(2, w)

        return carry

    lax.fori_loop(0, WORK, leaving, 0)

    def slab_done(r, carry):
        @pl.when(to_base + r != site)
        def _():
            for copy in slab_copies(r):
                copy.wait_send()

        return carry

    lax.fori_loop(0, PLANES, slab_done, 0)

    def spread_done(q, carry):
        sent = full.at[q, 0, pl.ds(0, SIDE - 1), 0]
        pltpu.make_async_copy(sent, sent, leg_ss.at[q]).wait()
        sent = full.at[q, pl.ds(0, SIDE - 1), :, 0]
        pltpu.make_async_copy(sent, sent, orb_ss.at[q]).wait()
        for o in range(ORB):
            forward(q, o).wait_send()
        return carry

    lax.fori_loop(0, depth, spread_done, 0)
    vec_sent = starts.at[pl.ds(0, chips - 1)]
    pltpu.make_async_copy(vec_sent, vec_sent, vec_ss).wait()

    def messages_done(q, carry):
        messages(q, False)
        results(q, False)
        return carry

    lax.fori_loop(0, depth, messages_done, 0)


def solution(mesh):
    sites, terms = mesh.shape["site"], mesh.shape["term"]
    chips = terms // 2

    def body(left_edge, mps, block_list, coupling, right_env, start_vector):
        shard = jnp.swapaxes(mps, 3, 4).reshape(ORB * 8, 4, N)
        start = jnp.swapaxes(start_vector[0], 1, 2)
        vmem = pl.BlockSpec(memory_space=pltpu.VMEM)
        anywhere = pl.BlockSpec(memory_space=pl.ANY)
        smem = pl.BlockSpec(memory_space=pltpu.SMEM)
        dma = pltpu.SemaphoreType.DMA
        env, state, energy = pl.pallas_call(
            functools.partial(kernel, sites, terms),
            out_shape=(
                jax.ShapeDtypeStruct((WORK, SEC, N, N), F32),
                jax.ShapeDtypeStruct((SEC, 4, N), F32),
                jax.ShapeDtypeStruct((8, N), F32),
            ),
            in_specs=[smem, smem, anywhere, anywhere, anywhere, anywhere],
            out_specs=(vmem, vmem, vmem),
            scratch_shapes=[
                pltpu.VMEM((WORK, SEC, N, N), F32),
                pltpu.VMEM((ORB * 8, 4, N), F32),
                pltpu.VMEM((WORK, SEC, N, N), F32),
                pltpu.VMEM((SEC, 4, N), F32),
                pltpu.VMEM((32 + SEC, 8, N), F32),
                pltpu.VMEM((32 + SEC, 8, N), F32),
                pltpu.VMEM((32 + SEC, 8, N), F32),
                pltpu.VMEM((DEEP, 16, 8, N), F32),
                pltpu.VMEM((8, N), F32),
                pltpu.VMEM((DEEP, 8, N), F32),
                pltpu.VMEM((DEEP, N, N), F32),
                pltpu.VMEM((DEEP, SIDE, SIDE, 2, 16, 8, N), F32),
                pltpu.VMEM((chips, SEC, 8, N), F32),
                pltpu.VMEM((DEEP, ORB, SEC, N, PHYS * N), BF16),
                pltpu.VMEM((DEEP, ORB, SEC, 2, N, PHYS * N), BF16),
                pltpu.VMEM((SEC, WORK * N, 2 * N), BF16),
                pltpu.VMEM((SEC, WORK * N, 2 * N), BF16),
                pltpu.VMEM((SEC, N, N), F32),
                pltpu.VMEM((DEEP, N + 8, N), F32),
                pltpu.VMEM((3, WORK, N + 8, N), F32),
                pltpu.VMEM((SEC, N, N), F32),
                pltpu.VMEM((2, terms, 8, N), F32),
                pltpu.VMEM((2, terms, 8, N), F32),
                pltpu.VMEM((2, 8, N), F32),
                pltpu.VMEM((2, terms, 8, N), F32),
                dma, dma, dma((PLANES,)), dma((DEEP,)), dma((PLANES,)), dma((DEEP,)),
                dma((DEEP,)), dma((DEEP, ORB)), dma((DEEP,)), dma((DEEP, ORB, SIDE - 1)), dma((DEEP, ORB)), dma((DEEP, ORB)),
                dma, dma, dma((3, DEEP)), dma((3, WORK)), dma((2,)), dma((2,)), dma((2,)), dma((2,)),
                dma((4,)), pltpu.SemaphoreType.REGULAR,
            ],
            compiler_params=pltpu.CompilerParams(
                collective_id=0, has_side_effects=True, vmem_limit_bytes=48 * 1024 * 1024
            ),
        )(block_list, coupling, left_edge, shard, right_env[0], start)
        return env[None], jnp.swapaxes(state, 1, 2)[None], energy[0, 0:1]

    in_specs = (
        P("term", None, None, None),
        P("site", None, None, None, "term"),
        P("site", None, None),
        P("term", "site", None),
        P("site", "term", None, None, None),
        P("site", None, None, "term"),
    )
    out_specs = (P("site", "term", None, None, None), P("site", None, None, "term"), P("site"))
    return jax.shard_map(body, mesh=mesh, in_specs=in_specs, out_specs=out_specs, check_vma=False)
```

```python
import functools

import jax
import jax.numpy as jnp
from jax import lax
from jax.experimental import pallas as pl
from jax.experimental.pallas import tpu as pltpu
from jax.sharding import PartitionSpec as P

ITERS = 4
STEP = 0.5
EPSILON = 1e-06
N = 128
ORB = 4
PHYS = 4
SEC = 2
WORK = 4
PLANES = 4
GROUPS = ((0, 3, 0, 4), (3, 3, 3, 6), (6, 4, 4, 7), (10, 6, 6, 9))
DEEP = max(group[1] for group in GROUPS)
SIDE = 4
MESH = pl.DeviceIdType.MESH
F32, BF16 = jnp.float32, jnp.bfloat16


def split(x):
    high = x.astype(BF16)
    return high, (x - high.astype(F32)).astype(BF16)


def dot(a, b):
    return lax.dot_general(a, b, (((1,), (0,)), ((), ())), preferred_element_type=F32)


def by_plane(plane, field):
    value = jnp.int32(GROUPS[0][field])
    for index, group in enumerate(GROUPS):
        value = jnp.where(plane >= index * PLANES, group[field], value)
    return value


def first_plane(segment):
    value = jnp.int32(0)
    for index, group in enumerate(GROUPS):
        value = jnp.where(segment >= group[0], index * PLANES, value)
    return value


def greetings(sites):
    carrier = {}
    for index, (first, depth, _, _) in enumerate(GROUPS):
        for segment in range(first, first + depth):
            carrier[segment] = index * PLANES
    early, late = set(), set()
    for segment, base in carrier.items():
        early |= {(segment, base + r) for r in range(PLANES)}
        for r in range(PLANES):
            late.add((base + r, segment))
            if segment + 1 < sites:
                late |= {(base + r, carrier[segment + 1] + r), (base + r, segment + 1)}
    early = {(a, b) for a, b in early if a != b}
    late = {(a, b) for a, b in late if a != b and (a, b) not in early}
    return {(b, a) for a, b in early} | late, {(b, a) for a, b in late}


def lookup(site, values):
    chosen = jnp.int32(0)
    for plane, value in enumerate(values):
        chosen = jnp.where(site == plane, value, chosen)
    return chosen


def kernel(
    sites,
    terms,
    perm_ref,
    coup_ref,
    left_ref,
    mps_ref,
    right_ref,
    start_ref,
    env_ref,
    state_ref,
    energy_ref,
    left_in,
    mps_in,
    right_in,
    start_in,
    mine,
    theirs,
    slab,
    slabs,
    coef,
    lanes,
    coefs,
    full,
    starts,
    weights_b,
    weights_t,
    enter_hl,
    right_hl,
    cur,
    tx,
    rx,
    vec,
    part,
    pieces,
    reduced,
    gathered,
    quotient,
    pair_ss,
    pair_rs,
    slab_ss,
    slab_rs,
    coef_ss,
    coef_rs,
    leg_ss,
    leg_rs,
    orb_ss,
    orb_rs,
    fwd_ss,
    fwd_rs,
    vec_ss,
    vec_rs,
    tx_sem,
    rx_sem,
    red_ss,
    red_rs,
    gat_ss,
    gat_rs,
    load_sem,
    answered,
):
    site = lax.axis_index("site")
    me = lax.axis_index("term")
    chip, core = me // 2, me % 2
    chips = terms // 2
    sibling = chip * 2 + (1 - core)
    last = sites - 1
    first, depth, ready, steps = (by_plane(site, field) for field in range(4))
    term = lax.rem(site, PLANES)
    x, y = chip % SIDE, chip // SIDE

    loads = [
        pltpu.make_async_copy(outside, inside, load_sem.at[index])
        for index, (outside, inside) in enumerate(
            ((mps_ref, mps_in), (start_ref, start_in), (left_ref, left_in), (right_ref, right_in))
        )
    ]
    for load in loads:
        load.start()

    def along_x(d):
        return {"term": (y * SIDE + lax.rem(x + d, SIDE)) * 2 + core}

    def along_y(d):
        return {"term": (lax.rem(y + d, SIDE) * SIDE + x) * 2 + core}

    barrier = pltpu.get_barrier_semaphore()
    for d in range(1, SIDE):
        for line in (along_x, along_y):
            pl.semaphore_signal(barrier, inc=1, device_id=line(d), device_id_type=MESH)
    pl.semaphore_signal(barrier, inc=1, device_id={"term": sibling}, device_id_type=MESH)
    entry, answers = greetings(sites)

    def signal_planes(pairs, semaphore):
        mask = lookup(site, [sum(1 << b for a, b in pairs if a == plane) for plane in range(sites)])

        def one(other, carry):
            @pl.when((mask >> other) % 2 == 1)
            def _():
                pl.semaphore_signal(semaphore, inc=1, device_id={"site": other}, device_id_type=MESH)

            return carry

        lax.fori_loop(0, sites, one, 0)

    def greeted(pairs):
        return lookup(site, [sum(1 for a, b in pairs if b == plane) for plane in range(sites)])

    signal_planes(entry, barrier)

    loads[0].wait()
    loads[1].wait()
    shard = mps_in[...]
    shard = jnp.concatenate([shard, shard], axis=1).reshape(ORB, 2, 4, 8, N)
    for h in range(2):
        mine[h * 16 : (h + 1) * 16] = shard[:, h].reshape(16, 8, N)
    own = start_in[...]
    mine[32 : 32 + SEC] = jnp.concatenate([own, own], axis=1)

    lane = lax.broadcasted_iota(jnp.int32, (8, N), 1)

    compact = jnp.zeros((8, N), F32)
    for w in range(WORK):
        for o in range(ORB):
            for p in range(PHYS):
                compact = jnp.where(lane == (w * ORB + o) * PHYS + p, coup_ref[w, o, p], compact)
    for o in range(ORB):
        for p in range(PHYS):
            for t in range(SEC):
                index = WORK * ORB * PHYS + (o * PHYS + p) * SEC + t
                compact = jnp.where(lane == index, perm_ref[o, p, t].astype(F32), compact)
    coef[...] = compact
    pl.semaphore_wait(barrier, 2 * (SIDE - 1) + 1 + greeted(entry))
    signal_planes(answers, answered)

    pair = pltpu.make_async_remote_copy(
        src_ref=mine, dst_ref=theirs, send_sem=pair_ss, recv_sem=pair_rs,
        device_id={"term": sibling}, device_id_type=MESH,
    )
    pair.start()
    pair.wait()
    half = lax.broadcasted_iota(jnp.int32, (32 + SEC, 8, N), 1) // 4
    slab[...] = jnp.where(half == core, mine[...], theirs[...])

    source = slab.at[pl.ds(core * 16, 16)]
    to_base = first_plane(site)

    place_of = site - by_plane(to_base, 0)

    def slab_copies(r):
        return [
            pltpu.make_async_remote_copy(
                src_ref=src, dst_ref=dst, send_sem=ss.at[r], recv_sem=rs.at[place_of],
                device_id={"site": to_base + r}, device_id_type=MESH,
            )
            for src, dst, ss, rs in (
                (source, slabs.at[place_of], slab_ss, slab_rs),
                (coef, lanes.at[place_of], coef_ss, coef_rs),
            )
        ]

    def slab_send(r, carry):
        @pl.when(to_base + r == site)
        def _():
            pltpu.make_async_copy(source, slabs.at[place_of], slab_rs.at[place_of]).start()
            pltpu.make_async_copy(coef, lanes.at[place_of], coef_rs.at[place_of]).start()

        @pl.when(to_base + r != site)
        def _():
            for copy in slab_copies(r):
                copy.start()

        return carry

    lax.fori_loop(0, PLANES, slab_send, 0)

    def tiles_of(o):
        return pl.ds(o * 4, 4)

    def row_of(q, o, r):
        return full.at[q, r, :, core, tiles_of(o)]

    def column_of(q, o, c):
        return full.at[q, :, c, core, tiles_of(o)]

    def first_leg(q, o):
        place = full.at[q, y, x, core, tiles_of(o)]
        tiles = slabs.at[q, tiles_of(o)]
        pltpu.make_async_copy(tiles, place, leg_rs.at[q, o]).start()
        for d in range(1, SIDE):
            pltpu.make_async_remote_copy(
                src_ref=tiles, dst_ref=place, send_sem=leg_ss.at[q], recv_sem=leg_rs.at[q, o],
                device_id=(along_x, along_y)[o % 2](d), device_id_type=MESH,
            ).start()

    def second_leg(q, o):
        line = row_of(q, o, y) if o % 2 == 0 else column_of(q, o, x)
        pltpu.make_async_copy(line, line, leg_rs.at[q, o]).wait()
        for d in range(1, SIDE):
            pltpu.make_async_remote_copy(
                src_ref=line, dst_ref=line, send_sem=orb_ss.at[q], recv_sem=orb_rs.at[q, o, d - 1],
                device_id=(along_y, along_x)[o % 2](d), device_id_type=MESH,
            ).start()

    def arrived(q, o, parity):
        for d in range(1, SIDE):
            if parity == 0:
                line = row_of(q, o, lax.rem(y + SIDE - d, SIDE))
            else:
                line = column_of(q, o, lax.rem(x + SIDE - d, SIDE))
            pltpu.make_async_copy(line, line, orb_rs.at[q, o, d - 1]).wait()

    def forward(q, o):
        tiles = full.at[q, :, :, core, tiles_of(o)]
        return pltpu.make_async_remote_copy(
            src_ref=tiles, dst_ref=tiles, send_sem=fwd_ss.at[q, o], recv_sem=fwd_rs.at[q, o],
            device_id={"term": sibling}, device_id_type=MESH,
        )

    row = lax.broadcasted_iota(jnp.int32, (N, N), 0)
    column = lax.broadcasted_iota(jnp.int32, (N, N), 1)

    def turn(i):
        return lax.rem(i + (site - term - first), depth)

    def gather_step(i):
        @pl.when(i < depth)
        def _():
            q = turn(i)
            pltpu.make_async_copy(slabs.at[q], slabs.at[q], slab_rs.at[q]).wait()
            pltpu.make_async_copy(lanes.at[q], lanes.at[q], coef_rs.at[q]).wait()
            for o in range(ORB):
                first_leg(q, o)
            rows = jnp.broadcast_to(lanes[q, 0:1], (N, N)).T
            coefs[q] = jnp.where(row < WORK * ORB * PHYS, jnp.sqrt(rows), rows)

        @pl.when(jnp.logical_and(i >= 1, i < depth + 1))
        def _():
            for o in range(ORB):
                second_leg(turn(i - 1), o)

        @pl.when(jnp.logical_and(i >= 3, i < depth + 3))
        def _():
            for o in range(ORB):
                arrived(turn(i - 3), o, o % 2)
                forward(turn(i - 3), o).start()

    def gather_loop(i, carry):
        gather_step(i)
        return carry

    lax.fori_loop(0, steps, gather_loop, 0)

    vec_source = slab.at[pl.ds(32, SEC)]

    def side_work():
        pltpu.make_async_copy(vec_source, starts.at[chip], vec_rs).start()

        def vec_copy(d, c):
            peer = lax.rem(chip + d, chips) * 2 + core
            pltpu.make_async_remote_copy(
                src_ref=vec_source, dst_ref=starts.at[chip], send_sem=vec_ss, recv_sem=vec_rs,
                device_id={"term": peer}, device_id_type=MESH,
            ).start()
            return c

        lax.fori_loop(1, chips, vec_copy, 0)

        loads[3].wait()

        def prepare_right(w, carry):
            for s in range(SEC):
                high, low = split(right_in[w, s])
                right_hl[s, pl.ds(w * N, N), 0:N] = high
                right_hl[s, pl.ds(w * N, N), N : 2 * N] = low
            return carry

        lax.fori_loop(0, WORK, prepare_right, 0)

    pl.when(ready > 0)(side_work)

    def coefficient(q, index):
        return coefs[q, pl.ds(index, 1)]

    def sector(q, o, p, t):
        return coefficient(q, WORK * ORB * PHYS + (o * PHYS + p) * SEC + t)

    def prepare(q, o):
        there = full.at[q, :, :, 1 - core, tiles_of(o)]
        pltpu.make_async_copy(there, there, fwd_rs.at[q, o]).wait()
        for p in range(PHYS):
            root = coefficient(q, (term * ORB + o) * PHYS + p)
            blocks = [full[q, :, :, p // 2, o * 4 + (p % 2) * SEC + t].reshape(N, N) * root for t in range(SEC)]
            columns = slice(p * N, (p + 1) * N)
            for t in range(SEC):
                high, low = split(blocks[t])
                weights_t[q, o, t, 0, :, columns] = high * BF16(0.5)
                weights_t[q, o, t, 1, :, columns] = low
            source_of_first = sector(q, o, p, 0)
            for s in range(SEC):
                weights_b[q, o, s, :, columns] = jnp.where(source_of_first == s, blocks[0], blocks[1]).T.astype(BF16)

    def orbital(q, o):
        sides = [jnp.concatenate(split(cur[s]), axis=1) for s in range(SEC)]
        pairs = [slice(g * 2 * N, (g + 1) * 2 * N) for g in range(PHYS // 2)]
        moved = []
        for pair_columns in pairs:
            blocks = [weights_b[q, o, s, :, pair_columns] for s in range(SEC)]
            moved.append([dot(sides[s], jnp.concatenate([blocks[s], blocks[s]], axis=0)) for s in range(SEC)])
        totals = [None] * SEC
        for g, pair_columns in enumerate(pairs):
            for t in range(SEC):
                highs, lows = [], []
                for within in range(2):
                    columns = slice(within * N, (within + 1) * N)
                    chosen = sector(q, o, g * 2 + within, t) == 0
                    high, low = split(jnp.where(chosen, moved[g][0][:, columns], moved[g][1][:, columns]))
                    highs.append(high)
                    lows.append(low)
                high, low = jnp.concatenate(highs, axis=0), jnp.concatenate(lows, axis=0)
                wide = dot(weights_t[q, o, t, 0, :, pair_columns], jnp.concatenate([high, low], axis=1))
                y = wide[:, :N] + wide[:, N:] + dot(weights_t[q, o, t, 1, :, pair_columns], high)
                totals[t] = y if g == 0 else totals[t] + y
        for t in range(SEC):
            cur[t] = totals[t] + totals[t].T

    def unpack(kind, w):
        packed = rx[kind, w, 0:N]
        flipped = packed.T
        diagonal = rx[kind, w, N : N + 1]
        return (
            jnp.where(row <= column, packed, flipped),
            jnp.where(row > column, packed, jnp.where(row < column, flipped, diagonal)),
        )

    def message(kind, w, slot, plane):
        return pltpu.make_async_remote_copy(
            src_ref=tx.at[slot], dst_ref=rx.at[kind, w], send_sem=tx_sem.at[kind, slot], recv_sem=rx_sem.at[kind, w],
            device_id={"site": plane}, device_id_type=MESH,
        )

    def received(kind, w):
        pltpu.make_async_copy(rx.at[kind, w], rx.at[kind, w], rx_sem.at[kind, w]).wait()

    def act(copy, start):
        if start:
            copy.start()
        else:
            copy.wait_send()

    def messages(q, start):
        segment = first + q
        after = lax.rem(segment + 1, sites)
        goes_on = jnp.logical_and(q == depth - 1, segment < last)
        pl.when(goes_on)(lambda: act(message(0, term, q, first_plane(after) + term), start))
        pl.when(jnp.logical_and(segment < last, after != site))(lambda: act(message(1, term, q, after), start))
        if start:

            @pl.when(jnp.logical_and(segment < last, after == site))
            def _():
                pltpu.make_async_copy(tx.at[q], rx.at[1, term], rx_sem.at[1, term]).start()

    def results(q, start):
        pl.when(first + q != site)(lambda: act(message(2, term, q, first + q), start))

    def early(index, carry):
        prepare(turn(index // ORB), index % ORB)
        return carry

    lax.fori_loop(0, ready * ORB, early, 0)
    loads[2].wait()
    pl.semaphore_wait(answered, greeted(answers))

    @pl.when(first == 0)
    def _():
        cur[...] = left_in[term]

    @pl.when(first > 0)
    def _():
        received(0, term)
        cur[0], cur[1] = unpack(0, term)

    def one_segment(q, c):
        pl.when(q + 3 >= steps)(lambda: gather_step(q + 3))

        def inline(o, cc):
            prepare(q, o)
            return cc

        lax.fori_loop(0, jnp.where(q >= ready, ORB, 0), inline, 0)
        for o in range(ORB):
            orbital(q, o)
        tx[q, 0:N] = jnp.where(row <= column, cur[0], cur[1])
        diagonal = jnp.sum(jnp.where(row == column, cur[1], 0.0), axis=0, keepdims=True)
        tx[q, N : N + 8] = jnp.broadcast_to(diagonal, (8, N))
        messages(q, True)

        @pl.when(first + q == site)
        def _():
            env_ref[term] = cur[...]

        return c

    lax.fori_loop(0, depth, one_segment, 0)

    def results_start(q, carry):
        results(q, True)
        return carry

    lax.fori_loop(0, depth, results_start, 0)
    pl.when(ready == 0)(side_work)

    def entering(w, carry):
        pl.when(site > 0)(lambda: received(1, w))

        def keep(blocks):
            for s in range(SEC):
                high, low = split(blocks[s])
                enter_hl[s, pl.ds(w * N, N), 0:N] = high
                enter_hl[s, pl.ds(w * N, N), N : 2 * N] = low

        pl.when(site == 0)(lambda: keep((left_in[w, 0], left_in[w, 1])))
        pl.when(site > 0)(lambda: keep(unpack(1, w)))
        return carry

    lax.fori_loop(0, WORK, entering, 0)

    entries = SEC * N * N
    pltpu.make_async_copy(starts, starts, vec_rs).wait()
    u = [starts[:, s].reshape(N, N) for s in range(SEC)]
    scale = jnp.sqrt((jnp.sum(u[0] * u[0]) + jnp.sum(u[1] * u[1])) / entries + EPSILON)
    for s in range(SEC):
        vec[s] = u[s] / scale

    def total_of(values):
        return jnp.sum(values, axis=(0, 1, 2), keepdims=True)

    offsets = sorted(
        ((a, b, c) for a in range(SIDE) for b in range(SIDE) for c in range(2) if (a, b, c) != (0, 0, 0)),
        key=lambda abc: -min(abc[0], SIDE - abc[0]) - min(abc[1], SIDE - abc[1]),
    )
    far_first = [
        (lax.rem(y + a, SIDE) * SIDE + lax.rem(x + b, SIDE)) * 2 + (core if c == 0 else 1 - core) for a, b, c in offsets
    ]

    def iteration(it, carry):
        slot = lax.rem(it, 2)
        for s in range(SEC):
            high, low = split(vec[s])
            sides = jnp.concatenate(
                [jnp.concatenate([high, low], axis=1), jnp.concatenate([high, jnp.zeros_like(high)], axis=1)], axis=0
            )
            wide = dot(right_hl[s], sides)
            product = wide[:, :N] + wide[:, N:]
            high, low = split(product)
            high = jnp.concatenate([high[w * N : (w + 1) * N] for w in range(WORK)], axis=1)
            low = jnp.concatenate([low[w * N : (w + 1) * N] for w in range(WORK)], axis=1)
            wide = dot(high, enter_hl[s])
            total = wide[:, :N] + wide[:, N:] + dot(low, enter_hl[s, :, 0:N])
            part[slot, pl.ds(s * (N // 8), N // 8)] = total.reshape(N // 8, 8, N)

        pltpu.make_async_copy(part.at[slot, me], pieces.at[slot, me], red_rs.at[slot]).start()

        for peer in far_first:
            pltpu.make_async_remote_copy(
                src_ref=part.at[slot, peer], dst_ref=pieces.at[slot, me], send_sem=red_ss.at[slot],
                recv_sem=red_rs.at[slot], device_id={"term": peer}, device_id_type=MESH,
            ).start()

        old = vec[...]
        square = total_of(old * old)

        pltpu.make_async_copy(pieces.at[slot], pieces.at[slot], red_rs.at[slot]).wait()
        reduced[slot] = jnp.sum(pieces[slot], axis=0) * (1.0 / (WORK * terms))
        pltpu.make_async_copy(reduced.at[slot], gathered.at[slot, me], gat_rs.at[slot]).start()

        for peer in far_first:
            pltpu.make_async_remote_copy(
                src_ref=reduced.at[slot], dst_ref=gathered.at[slot, me], send_sem=gat_ss.at[slot],
                recv_sem=gat_rs.at[slot], device_id={"term": peer}, device_id_type=MESH,
            ).start()

        pltpu.make_async_copy(gathered.at[slot], gathered.at[slot], gat_rs.at[slot]).wait()
        sent = pieces.at[slot, pl.ds(0, terms - 1)]
        pltpu.make_async_copy(sent, sent, red_ss.at[slot]).wait()
        pltpu.make_async_copy(sent, sent, gat_ss.at[slot]).wait()

        image = gathered[slot].reshape(SEC, N, N)
        rayleigh = total_of(old * image) / square
        corrected = old - STEP * (image - rayleigh * old)
        vec[...] = corrected / jnp.sqrt(total_of(corrected * corrected) / entries + EPSILON)
        quotient[...] = jnp.broadcast_to(rayleigh[0], (8, N))
        return carry

    lax.fori_loop(0, ITERS, iteration, 0)
    energy_ref[0, 0] = quotient[0, 0]
    for s in range(SEC):
        rows = vec[s, pl.ds(pl.multiple_of(chip * 8, 8), 8)]
        state_ref[s] = jnp.where(core == 0, rows[0:4], rows[4:8])

    def leaving(w, carry):
        @pl.when(first_plane(site) + w != site)
        def _():
            received(2, w)
            env_ref[w, 0], env_ref[w, 1] = unpack(2, w)

        return carry

    lax.fori_loop(0, WORK, leaving, 0)

    def slab_done(r, carry):
        @pl.when(to_base + r != site)
        def _():
            for copy in slab_copies(r):
                copy.wait_send()

        return carry

    lax.fori_loop(0, PLANES, slab_done, 0)

    def spread_done(q, carry):
        sent = full.at[q, 0, pl.ds(0, SIDE - 1), 0]
        pltpu.make_async_copy(sent, sent, leg_ss.at[q]).wait()
        sent = full.at[q, pl.ds(0, SIDE - 1), :, 0]
        pltpu.make_async_copy(sent, sent, orb_ss.at[q]).wait()
        for o in range(ORB):
            forward(q, o).wait_send()
        return carry

    lax.fori_loop(0, depth, spread_done, 0)
    vec_sent = starts.at[pl.ds(0, chips - 1)]
    pltpu.make_async_copy(vec_sent, vec_sent, vec_ss).wait()

    def messages_done(q, carry):
        messages(q, False)
        results(q, False)
        return carry

    lax.fori_loop(0, depth, messages_done, 0)


def solution(mesh):
    sites, terms = mesh.shape["site"], mesh.shape["term"]
    chips = terms // 2

    def body(left_edge, mps, block_list, coupling, right_env, start_vector):
        shard = jnp.swapaxes(mps, 3, 4).reshape(ORB * 8, 4, N)
        start = jnp.swapaxes(start_vector[0], 1, 2)
        vmem = pl.BlockSpec(memory_space=pltpu.VMEM)
        anywhere = pl.BlockSpec(memory_space=pltpu.HBM)
        smem = pl.BlockSpec(memory_space=pltpu.SMEM)
        dma = pltpu.SemaphoreType.DMA
        env, state, energy = pl.pallas_call(
            functools.partial(kernel, sites, terms),
            out_shape=(
                jax.ShapeDtypeStruct((WORK, SEC, N, N), F32),
                jax.ShapeDtypeStruct((SEC, 4, N), F32),
                jax.ShapeDtypeStruct((1, 1), F32),
            ),
            in_specs=[smem, smem, anywhere, anywhere, anywhere, anywhere],
            out_specs=(vmem, vmem, smem),
            scratch_shapes=[
                pltpu.VMEM((WORK, SEC, N, N), F32),
                pltpu.VMEM((ORB * 8, 4, N), F32),
                pltpu.VMEM((WORK, SEC, N, N), F32),
                pltpu.VMEM((SEC, 4, N), F32),
                pltpu.VMEM((32 + SEC, 8, N), F32),
                pltpu.VMEM((32 + SEC, 8, N), F32),
                pltpu.VMEM((32 + SEC, 8, N), F32),
                pltpu.VMEM((DEEP, 16, 8, N), F32),
                pltpu.VMEM((8, N), F32),
                pltpu.VMEM((DEEP, 8, N), F32),
                pltpu.VMEM((DEEP, N, N), F32),
                pltpu.VMEM((DEEP, SIDE, SIDE, 2, 16, 8, N), F32),
                pltpu.VMEM((chips, SEC, 8, N), F32),
                pltpu.VMEM((DEEP, ORB, SEC, N, PHYS * N), BF16),
                pltpu.VMEM((DEEP, ORB, SEC, 2, N, PHYS * N), BF16),
                pltpu.VMEM((SEC, WORK * N, 2 * N), BF16),
                pltpu.VMEM((SEC, WORK * N, 2 * N), BF16),
                pltpu.VMEM((SEC, N, N), F32),
                pltpu.VMEM((DEEP, N + 8, N), F32),
                pltpu.VMEM((3, WORK, N + 8, N), F32),
                pltpu.VMEM((SEC, N, N), F32),
                pltpu.VMEM((2, terms, 8, N), F32),
                pltpu.VMEM((2, terms, 8, N), F32),
                pltpu.VMEM((2, 8, N), F32),
                pltpu.VMEM((2, terms, 8, N), F32),
                pltpu.VMEM((8, N), F32),
                dma, dma, dma((PLANES,)), dma((DEEP,)), dma((PLANES,)), dma((DEEP,)),
                dma((DEEP,)), dma((DEEP, ORB)), dma((DEEP,)), dma((DEEP, ORB, SIDE - 1)), dma((DEEP, ORB)), dma((DEEP, ORB)),
                dma, dma, dma((3, DEEP)), dma((3, WORK)), dma((2,)), dma((2,)), dma((2,)), dma((2,)),
                dma((4,)), pltpu.SemaphoreType.REGULAR,
            ],
            compiler_params=pltpu.CompilerParams(
                collective_id=0, has_side_effects=True, vmem_limit_bytes=(64 << 20) - (1 << 19)
            ),
        )(block_list, coupling, left_edge, shard, right_env[0], start)
        return env[None], jnp.swapaxes(state, 1, 2)[None], energy.reshape(1)

    in_specs = (
        P("term", None, None, None),
        P("site", None, None, None, "term"),
        P("site", None, None),
        P("term", "site", None),
        P("site", "term", None, None, None),
        P("site", None, None, "term"),
    )
    out_specs = (P("site", "term", None, None, None), P("site", None, None, "term"), P("site"))
    return jax.shard_map(body, mesh=mesh, in_specs=in_specs, out_specs=out_specs, check_vma=False)
```

```python
import functools

import jax
import jax.numpy as jnp
from jax import lax
from jax.experimental import pallas as pl
from jax.experimental.pallas import tpu as pltpu
from jax.sharding import PartitionSpec as P

ITERS = 4
STEP = 0.5
EPSILON = 1e-06
N = 128
ORB = 4
PHYS = 4
SEC = 2
WORK = 4
PLANES = 4
GROUPS = ((0, 3, 0, 4), (3, 3, 3, 7), (6, 4, 4, 8), (10, 6, 6, 10))
DEEP = max(group[1] for group in GROUPS)
SIDE = 4
MESH = pl.DeviceIdType.MESH
F32, BF16 = jnp.float32, jnp.bfloat16


def split(x):
    high = x.astype(BF16)
    return high, (x - high.astype(F32)).astype(BF16)


def dot(a, b):
    return lax.dot_general(a, b, (((1,), (0,)), ((), ())), preferred_element_type=F32)


def by_plane(plane, field):
    value = jnp.int32(GROUPS[0][field])
    for index, group in enumerate(GROUPS):
        value = jnp.where(plane >= index * PLANES, group[field], value)
    return value


def first_plane(segment):
    value = jnp.int32(0)
    for index, group in enumerate(GROUPS):
        value = jnp.where(segment >= group[0], index * PLANES, value)
    return value


def greetings(sites):
    carrier = {}
    for index, (first, depth, _, _) in enumerate(GROUPS):
        for segment in range(first, first + depth):
            carrier[segment] = index * PLANES
    early, late = set(), set()
    for segment, base in carrier.items():
        early |= {(segment, base + r) for r in range(PLANES)}
        for r in range(PLANES):
            late.add((base + r, segment))
            if segment + 1 < sites:
                late |= {(base + r, carrier[segment + 1] + r), (base + r, segment + 1)}
    early = {(a, b) for a, b in early if a != b}
    late = {(a, b) for a, b in late if a != b and (a, b) not in early}
    return {(b, a) for a, b in early} | late, {(b, a) for a, b in late}


def lookup(site, values):
    chosen = jnp.int32(0)
    for plane, value in enumerate(values):
        chosen = jnp.where(site == plane, value, chosen)
    return chosen


def kernel(
    sites,
    terms,
    perm_ref,
    coup_ref,
    left_ref,
    mps_ref,
    right_ref,
    start_ref,
    env_ref,
    state_ref,
    energy_ref,
    left_in,
    mps_in,
    right_in,
    start_in,
    mine,
    theirs,
    slab,
    slabs,
    coef,
    lanes,
    coefs,
    full,
    starts,
    weights_b,
    scales,
    weights_t,
    enter_hl,
    right_hl,
    cur,
    tx,
    rx,
    vec,
    part,
    pieces,
    reduced,
    gathered,
    quotient,
    pair_ss,
    pair_rs,
    slab_ss,
    slab_rs,
    coef_ss,
    coef_rs,
    leg_ss,
    leg_rs,
    orb_ss,
    orb_rs,
    fwd_ss,
    fwd_rs,
    vec_ss,
    vec_rs,
    tx_sem,
    rx_sem,
    red_ss,
    red_rs,
    gat_ss,
    gat_rs,
    load_sem,
    answered,
):
    site = lax.axis_index("site")
    me = lax.axis_index("term")
    chip, core = me // 2, me % 2
    chips = terms // 2
    sibling = chip * 2 + (1 - core)
    last = sites - 1
    first, depth, ready, steps = (by_plane(site, field) for field in range(4))
    term = lax.rem(site, PLANES)
    x, y = chip % SIDE, chip // SIDE

    loads = [
        pltpu.make_async_copy(outside, inside, load_sem.at[index])
        for index, (outside, inside) in enumerate(
            ((mps_ref, mps_in), (start_ref, start_in), (left_ref, left_in), (right_ref, right_in))
        )
    ]
    for load in loads:
        load.start()

    def along_x(d):
        return {"term": (y * SIDE + lax.rem(x + d, SIDE)) * 2 + core}

    def along_y(d):
        return {"term": (lax.rem(y + d, SIDE) * SIDE + x) * 2 + core}

    barrier = pltpu.get_barrier_semaphore()
    for d in range(1, SIDE):
        for line in (along_x, along_y):
            pl.semaphore_signal(barrier, inc=1, device_id=line(d), device_id_type=MESH)
    pl.semaphore_signal(barrier, inc=1, device_id={"term": sibling}, device_id_type=MESH)
    entry, answers = greetings(sites)

    def signal_planes(pairs, semaphore):
        mask = lookup(site, [sum(1 << b for a, b in pairs if a == plane) for plane in range(sites)])

        def one(other, carry):
            @pl.when((mask >> other) % 2 == 1)
            def _():
                pl.semaphore_signal(semaphore, inc=1, device_id={"site": other}, device_id_type=MESH)

            return carry

        lax.fori_loop(0, sites, one, 0)

    def greeted(pairs):
        return lookup(site, [sum(1 for a, b in pairs if b == plane) for plane in range(sites)])

    signal_planes(entry, barrier)

    loads[0].wait()
    loads[1].wait()
    shard = mps_in[...]
    shard = jnp.concatenate([shard, shard], axis=1).reshape(ORB, 2, 4, 8, N)
    for h in range(2):
        mine[h * 16 : (h + 1) * 16] = shard[:, h].reshape(16, 8, N)
    own = start_in[...]
    mine[32 : 32 + SEC] = jnp.concatenate([own, own], axis=1)

    lane = lax.broadcasted_iota(jnp.int32, (8, N), 1)

    compact = jnp.zeros((8, N), F32)
    for w in range(WORK):
        for o in range(ORB):
            for p in range(PHYS):
                compact = jnp.where(lane == (w * ORB + o) * PHYS + p, coup_ref[w, o, p], compact)
    for o in range(ORB):
        for p in range(PHYS):
            for t in range(SEC):
                index = WORK * ORB * PHYS + (o * PHYS + p) * SEC + t
                compact = jnp.where(lane == index, perm_ref[o, p, t].astype(F32), compact)
    coef[...] = compact
    pl.semaphore_wait(barrier, 2 * (SIDE - 1) + 1 + greeted(entry))
    signal_planes(answers, answered)

    pair = pltpu.make_async_remote_copy(
        src_ref=mine, dst_ref=theirs, send_sem=pair_ss, recv_sem=pair_rs,
        device_id={"term": sibling}, device_id_type=MESH,
    )
    pair.start()
    pair.wait()
    half = lax.broadcasted_iota(jnp.int32, (32 + SEC, 8, N), 1) // 4
    slab[...] = jnp.where(half == core, mine[...], theirs[...])

    source = slab.at[pl.ds(core * 16, 16)]
    to_base = first_plane(site)

    place_of = site - by_plane(to_base, 0)

    def slab_copies(r):
        return [
            pltpu.make_async_remote_copy(
                src_ref=src, dst_ref=dst, send_sem=ss.at[r], recv_sem=rs.at[place_of],
                device_id={"site": to_base + r}, device_id_type=MESH,
            )
            for src, dst, ss, rs in (
                (source, slabs.at[place_of], slab_ss, slab_rs),
                (coef, lanes.at[place_of], coef_ss, coef_rs),
            )
        ]

    def slab_send(r, carry):
        @pl.when(to_base + r == site)
        def _():
            pltpu.make_async_copy(source, slabs.at[place_of], slab_rs.at[place_of]).start()
            pltpu.make_async_copy(coef, lanes.at[place_of], coef_rs.at[place_of]).start()

        @pl.when(to_base + r != site)
        def _():
            for copy in slab_copies(r):
                copy.start()

        return carry

    lax.fori_loop(0, PLANES, slab_send, 0)

    def tiles_of(o):
        return pl.ds(o * 4, 4)

    def row_of(q, o, r):
        return full.at[q, r, :, core, tiles_of(o)]

    def column_of(q, o, c):
        return full.at[q, :, c, core, tiles_of(o)]

    def first_leg(q, o):
        place = full.at[q, y, x, core, tiles_of(o)]
        tiles = slabs.at[q, tiles_of(o)]
        pltpu.make_async_copy(tiles, place, leg_rs.at[q, o]).start()
        for d in range(1, SIDE):
            pltpu.make_async_remote_copy(
                src_ref=tiles, dst_ref=place, send_sem=leg_ss.at[q], recv_sem=leg_rs.at[q, o],
                device_id=(along_x, along_y)[o % 2](d), device_id_type=MESH,
            ).start()

    def second_leg(q, o):
        line = row_of(q, o, y) if o % 2 == 0 else column_of(q, o, x)
        pltpu.make_async_copy(line, line, leg_rs.at[q, o]).wait()
        for d in range(1, SIDE):
            pltpu.make_async_remote_copy(
                src_ref=line, dst_ref=line, send_sem=orb_ss.at[q], recv_sem=orb_rs.at[q, o, d - 1],
                device_id=(along_y, along_x)[o % 2](d), device_id_type=MESH,
            ).start()

    def arrived(q, o, parity):
        for d in range(1, SIDE):
            if parity == 0:
                line = row_of(q, o, lax.rem(y + SIDE - d, SIDE))
            else:
                line = column_of(q, o, lax.rem(x + SIDE - d, SIDE))
            pltpu.make_async_copy(line, line, orb_rs.at[q, o, d - 1]).wait()

    def forward(q, o):
        tiles = full.at[q, :, :, core, tiles_of(o)]
        return pltpu.make_async_remote_copy(
            src_ref=tiles, dst_ref=tiles, send_sem=fwd_ss.at[q, o], recv_sem=fwd_rs.at[q, o],
            device_id={"term": sibling}, device_id_type=MESH,
        )

    row = lax.broadcasted_iota(jnp.int32, (N, N), 0)
    column = lax.broadcasted_iota(jnp.int32, (N, N), 1)

    def turn(i):
        return lax.rem(i + (site - term - first), depth)

    def gather_step(i):
        @pl.when(i < depth)
        def _():
            q = turn(i)
            pltpu.make_async_copy(slabs.at[q], slabs.at[q], slab_rs.at[q]).wait()
            pltpu.make_async_copy(lanes.at[q], lanes.at[q], coef_rs.at[q]).wait()
            for o in range(ORB):
                first_leg(q, o)
            rows = jnp.broadcast_to(lanes[q, 0:1], (N, N)).T
            coefs[q] = jnp.where(row < WORK * ORB * PHYS, jnp.sqrt(rows), rows)

        @pl.when(jnp.logical_and(i >= 1, i < depth + 1))
        def _():
            for o in range(ORB):
                second_leg(turn(i - 1), o)

        @pl.when(jnp.logical_and(i >= 3, i < depth + 3))
        def _():
            for o in range(ORB):
                arrived(turn(i - 3), o, o % 2)
                forward(turn(i - 3), o).start()

    vec_source = slab.at[pl.ds(32, SEC)]

    def side_work():
        pltpu.make_async_copy(vec_source, starts.at[chip], vec_rs).start()

        def vec_copy(d, c):
            peer = lax.rem(chip + d, chips) * 2 + core
            pltpu.make_async_remote_copy(
                src_ref=vec_source, dst_ref=starts.at[chip], send_sem=vec_ss, recv_sem=vec_rs,
                device_id={"term": peer}, device_id_type=MESH,
            ).start()
            return c

        lax.fori_loop(1, chips, vec_copy, 0)

        loads[3].wait()

        def prepare_right(w, carry):
            for s in range(SEC):
                high, low = split(right_in[w, s])
                right_hl[s, pl.ds(w * N, N), 0:N] = high
                right_hl[s, pl.ds(w * N, N), N : 2 * N] = low
            return carry

        lax.fori_loop(0, WORK, prepare_right, 0)


    def coefficient(q, index):
        return coefs[q, pl.ds(index, 1)]

    def sector(q, o, p, t):
        return coefficient(q, WORK * ORB * PHYS + (o * PHYS + p) * SEC + t)

    def prepare(q, o):
        there = full.at[q, :, :, 1 - core, tiles_of(o)]
        pltpu.make_async_copy(there, there, fwd_rs.at[q, o]).wait()
        for p in range(PHYS):
            root = coefficient(q, (term * ORB + o) * PHYS + p)
            columns = slice(p * N, (p + 1) * N)
            rounded, scale = [], []
            for t in range(SEC):
                block = (full[q, :, :, p // 2, o * 4 + (p % 2) * SEC + t].reshape(N, N) * root).T
                size = jnp.maximum(jnp.max(jnp.abs(block), axis=0, keepdims=True) * (128.0 / 255.0), 1e-30)
                near = (block * (1.0 / size)).astype(BF16).astype(F32)
                high, low = split((block - (near * size) * 0.5).T)
                weights_t[q, o, t, 0, :, columns] = high
                weights_t[q, o, t, 1, :, columns] = low
                rounded.append(near)
                scale.append(size)
            source_of_first = sector(q, o, p, 0)
            for s in range(SEC):
                weights_b[q, o, s, :, columns] = jnp.where(source_of_first == s, rounded[0], rounded[1]).astype(BF16)
                scales[q, o, s, 0:1, columns] = jnp.where(source_of_first == s, scale[0], scale[1])

    def orbital(q, o):
        sides = [jnp.concatenate(split(cur[s]), axis=1) for s in range(SEC)]
        pairs = [slice(g * 2 * N, (g + 1) * 2 * N) for g in range(PHYS // 2)]
        moved = []
        for pair_columns in pairs:
            blocks = [weights_b[q, o, s, :, pair_columns] for s in range(SEC)]
            moved.append(
                [
                    dot(sides[s], jnp.concatenate([blocks[s], blocks[s]], axis=0)) * scales[q, o, s, 0:1, pair_columns]
                    for s in range(SEC)
                ]
            )
        totals = [None] * SEC
        for g, pair_columns in enumerate(pairs):
            for t in range(SEC):
                highs, lows = [], []
                for within in range(2):
                    columns = slice(within * N, (within + 1) * N)
                    chosen = sector(q, o, g * 2 + within, t) == 0
                    high, low = split(jnp.where(chosen, moved[g][0][:, columns], moved[g][1][:, columns]))
                    highs.append(high)
                    lows.append(low)
                high, low = jnp.concatenate(highs, axis=0), jnp.concatenate(lows, axis=0)
                wide = dot(weights_t[q, o, t, 0, :, pair_columns], jnp.concatenate([high, low], axis=1))
                y = wide[:, :N] + wide[:, N:] + dot(weights_t[q, o, t, 1, :, pair_columns], high)
                totals[t] = y if g == 0 else totals[t] + y
        for t in range(SEC):
            cur[t] = totals[t] + totals[t].T

    def unpack(kind, w):
        packed = rx[kind, w, 0:N]
        flipped = packed.T
        diagonal = rx[kind, w, N : N + 1]
        return (
            jnp.where(row <= column, packed, flipped),
            jnp.where(row > column, packed, jnp.where(row < column, flipped, diagonal)),
        )

    def message(kind, w, slot, plane):
        return pltpu.make_async_remote_copy(
            src_ref=tx.at[slot], dst_ref=rx.at[kind, w], send_sem=tx_sem.at[kind, slot], recv_sem=rx_sem.at[kind, w],
            device_id={"site": plane}, device_id_type=MESH,
        )

    def received(kind, w):
        pltpu.make_async_copy(rx.at[kind, w], rx.at[kind, w], rx_sem.at[kind, w]).wait()

    def act(copy, start):
        if start:
            copy.start()
        else:
            copy.wait_send()

    def messages(q, start):
        segment = first + q
        after = lax.rem(segment + 1, sites)
        goes_on = jnp.logical_and(q == depth - 1, segment < last)
        pl.when(goes_on)(lambda: act(message(0, term, q, first_plane(after) + term), start))
        pl.when(jnp.logical_and(segment < last, after != site))(lambda: act(message(1, term, q, after), start))
        if start:

            @pl.when(jnp.logical_and(segment < last, after == site))
            def _():
                pltpu.make_async_copy(tx.at[q], rx.at[1, term], rx_sem.at[1, term]).start()

    def results(q, start):
        pl.when(first + q != site)(lambda: act(message(2, term, q, first + q), start))

    def gather_loop(i, carry):
        gather_step(i)

        @pl.when(jnp.logical_and(ready > 0, i >= 4))
        def _():
            for o in range(ORB):
                prepare(turn(i - 4), o)

        pl.when(jnp.logical_and(ready > 0, i == 2))(side_work)
        return carry

    lax.fori_loop(0, steps, gather_loop, 0)
    loads[2].wait()
    pl.semaphore_wait(answered, greeted(answers))

    @pl.when(first == 0)
    def _():
        cur[...] = left_in[term]

    @pl.when(first > 0)
    def _():
        received(0, term)
        cur[0], cur[1] = unpack(0, term)

    def one_segment(q, c):
        pl.when(q + 3 >= steps)(lambda: gather_step(q + 3))

        def inline(o, cc):
            prepare(q, o)
            return cc

        lax.fori_loop(0, jnp.where(q >= ready, ORB, 0), inline, 0)
        for o in range(ORB):
            orbital(q, o)
        tx[q, 0:N] = jnp.where(row <= column, cur[0], cur[1])
        diagonal = jnp.sum(jnp.where(row == column, cur[1], 0.0), axis=0, keepdims=True)
        tx[q, N : N + 8] = jnp.broadcast_to(diagonal, (8, N))
        messages(q, True)

        @pl.when(first + q == site)
        def _():
            env_ref[term] = cur[...]

        return c

    lax.fori_loop(0, depth, one_segment, 0)

    def results_start(q, carry):
        results(q, True)
        return carry

    lax.fori_loop(0, depth, results_start, 0)
    pl.when(ready == 0)(side_work)

    def entering(w, carry):
        pl.when(site > 0)(lambda: received(1, w))

        def keep(blocks):
            for s in range(SEC):
                high, low = split(blocks[s])
                enter_hl[s, pl.ds(w * N, N), 0:N] = high
                enter_hl[s, pl.ds(w * N, N), N : 2 * N] = low

        pl.when(site == 0)(lambda: keep((left_in[w, 0], left_in[w, 1])))
        pl.when(site > 0)(lambda: keep(unpack(1, w)))
        return carry

    lax.fori_loop(0, WORK, entering, 0)

    entries = SEC * N * N
    pltpu.make_async_copy(starts, starts, vec_rs).wait()
    u = [starts[:, s].reshape(N, N) for s in range(SEC)]
    scale = jnp.sqrt((jnp.sum(u[0] * u[0]) + jnp.sum(u[1] * u[1])) / entries + EPSILON)
    for s in range(SEC):
        vec[s] = u[s] / scale

    def total_of(values):
        return jnp.sum(values, axis=(0, 1, 2), keepdims=True)

    offsets = sorted(
        ((a, b, c) for a in range(SIDE) for b in range(SIDE) for c in range(2) if (a, b, c) != (0, 0, 0)),
        key=lambda abc: -min(abc[0], SIDE - abc[0]) - min(abc[1], SIDE - abc[1]),
    )
    far_first = [
        (lax.rem(y + a, SIDE) * SIDE + lax.rem(x + b, SIDE)) * 2 + (core if c == 0 else 1 - core) for a, b, c in offsets
    ]

    def iteration(it, carry):
        slot = lax.rem(it, 2)
        for s in range(SEC):
            high, low = split(vec[s])
            sides = jnp.concatenate(
                [jnp.concatenate([high, low], axis=1), jnp.concatenate([high, jnp.zeros_like(high)], axis=1)], axis=0
            )
            wide = dot(right_hl[s], sides)
            product = wide[:, :N] + wide[:, N:]
            high, low = split(product)
            high = jnp.concatenate([high[w * N : (w + 1) * N] for w in range(WORK)], axis=1)
            low = jnp.concatenate([low[w * N : (w + 1) * N] for w in range(WORK)], axis=1)
            wide = dot(high, enter_hl[s])
            total = wide[:, :N] + wide[:, N:] + dot(low, enter_hl[s, :, 0:N])
            part[slot, pl.ds(s * (N // 8), N // 8)] = total.reshape(N // 8, 8, N)

        pltpu.make_async_copy(part.at[slot, me], pieces.at[slot, me], red_rs.at[slot]).start()

        for peer in far_first:
            pltpu.make_async_remote_copy(
                src_ref=part.at[slot, peer], dst_ref=pieces.at[slot, me], send_sem=red_ss.at[slot],
                recv_sem=red_rs.at[slot], device_id={"term": peer}, device_id_type=MESH,
            ).start()

        old = vec[...]
        square = total_of(old * old)

        pltpu.make_async_copy(pieces.at[slot], pieces.at[slot], red_rs.at[slot]).wait()
        reduced[slot] = jnp.sum(pieces[slot], axis=0) * (1.0 / (WORK * terms))
        pltpu.make_async_copy(reduced.at[slot], gathered.at[slot, me], gat_rs.at[slot]).start()

        for peer in far_first:
            pltpu.make_async_remote_copy(
                src_ref=reduced.at[slot], dst_ref=gathered.at[slot, me], send_sem=gat_ss.at[slot],
                recv_sem=gat_rs.at[slot], device_id={"term": peer}, device_id_type=MESH,
            ).start()

        pltpu.make_async_copy(gathered.at[slot], gathered.at[slot], gat_rs.at[slot]).wait()
        sent = pieces.at[slot, pl.ds(0, terms - 1)]
        pltpu.make_async_copy(sent, sent, red_ss.at[slot]).wait()
        pltpu.make_async_copy(sent, sent, gat_ss.at[slot]).wait()

        image = gathered[slot].reshape(SEC, N, N)
        rayleigh = total_of(old * image) / square
        corrected = old - STEP * (image - rayleigh * old)
        vec[...] = corrected / jnp.sqrt(total_of(corrected * corrected) / entries + EPSILON)
        quotient[...] = jnp.broadcast_to(rayleigh[0], (8, N))
        return carry

    lax.fori_loop(0, ITERS, iteration, 0)
    energy_ref[0, 0] = quotient[0, 0]
    for s in range(SEC):
        rows = vec[s, pl.ds(pl.multiple_of(chip * 8, 8), 8)]
        state_ref[s] = jnp.where(core == 0, rows[0:4], rows[4:8])

    def leaving(w, carry):
        @pl.when(first_plane(site) + w != site)
        def _():
            received(2, w)
            env_ref[w, 0], env_ref[w, 1] = unpack(2, w)

        return carry

    lax.fori_loop(0, WORK, leaving, 0)

    def slab_done(r, carry):
        @pl.when(to_base + r != site)
        def _():
            for copy in slab_copies(r):
                copy.wait_send()

        return carry

    lax.fori_loop(0, PLANES, slab_done, 0)

    def spread_done(q, carry):
        sent = full.at[q, 0, pl.ds(0, SIDE - 1), 0]
        pltpu.make_async_copy(sent, sent, leg_ss.at[q]).wait()
        sent = full.at[q, pl.ds(0, SIDE - 1), :, 0]
        pltpu.make_async_copy(sent, sent, orb_ss.at[q]).wait()
        for o in range(ORB):
            forward(q, o).wait_send()
        return carry

    lax.fori_loop(0, depth, spread_done, 0)
    vec_sent = starts.at[pl.ds(0, chips - 1)]
    pltpu.make_async_copy(vec_sent, vec_sent, vec_ss).wait()

    def messages_done(q, carry):
        messages(q, False)
        results(q, False)
        return carry

    lax.fori_loop(0, depth, messages_done, 0)


def solution(mesh):
    sites, terms = mesh.shape["site"], mesh.shape["term"]
    chips = terms // 2

    def body(left_edge, mps, block_list, coupling, right_env, start_vector):
        shard = jnp.swapaxes(mps, 3, 4).reshape(ORB * 8, 4, N)
        start = jnp.swapaxes(start_vector[0], 1, 2)
        vmem = pl.BlockSpec(memory_space=pltpu.VMEM)
        anywhere = pl.BlockSpec(memory_space=pltpu.HBM)
        smem = pl.BlockSpec(memory_space=pltpu.SMEM)
        dma = pltpu.SemaphoreType.DMA
        env, state, energy = pl.pallas_call(
            functools.partial(kernel, sites, terms),
            out_shape=(
                jax.ShapeDtypeStruct((WORK, SEC, N, N), F32),
                jax.ShapeDtypeStruct((SEC, 4, N), F32),
                jax.ShapeDtypeStruct((1, 1), F32),
            ),
            in_specs=[smem, smem, anywhere, anywhere, anywhere, anywhere],
            out_specs=(vmem, vmem, smem),
            scratch_shapes=[
                pltpu.VMEM((WORK, SEC, N, N), F32),
                pltpu.VMEM((ORB * 8, 4, N), F32),
                pltpu.VMEM((WORK, SEC, N, N), F32),
                pltpu.VMEM((SEC, 4, N), F32),
                pltpu.VMEM((32 + SEC, 8, N), F32),
                pltpu.VMEM((32 + SEC, 8, N), F32),
                pltpu.VMEM((32 + SEC, 8, N), F32),
                pltpu.VMEM((DEEP, 16, 8, N), F32),
                pltpu.VMEM((8, N), F32),
                pltpu.VMEM((DEEP, 8, N), F32),
                pltpu.VMEM((DEEP, N, N), F32),
                pltpu.VMEM((DEEP, SIDE, SIDE, 2, 16, 8, N), F32),
                pltpu.VMEM((chips, SEC, 8, N), F32),
                pltpu.VMEM((DEEP, ORB, SEC, N, PHYS * N), BF16),
                pltpu.VMEM((DEEP, ORB, SEC, 8, PHYS * N), F32),
                pltpu.VMEM((DEEP, ORB, SEC, 2, N, PHYS * N), BF16),
                pltpu.VMEM((SEC, WORK * N, 2 * N), BF16),
                pltpu.VMEM((SEC, WORK * N, 2 * N), BF16),
                pltpu.VMEM((SEC, N, N), F32),
                pltpu.VMEM((DEEP, N + 8, N), F32),
                pltpu.VMEM((3, WORK, N + 8, N), F32),
                pltpu.VMEM((SEC, N, N), F32),
                pltpu.VMEM((2, terms, 8, N), F32),
                pltpu.VMEM((2, terms, 8, N), F32),
                pltpu.VMEM((2, 8, N), F32),
                pltpu.VMEM((2, terms, 8, N), F32),
                pltpu.VMEM((8, N), F32),
                dma, dma, dma((PLANES,)), dma((DEEP,)), dma((PLANES,)), dma((DEEP,)),
                dma((DEEP,)), dma((DEEP, ORB)), dma((DEEP,)), dma((DEEP, ORB, SIDE - 1)), dma((DEEP, ORB)), dma((DEEP, ORB)),
                dma, dma, dma((3, DEEP)), dma((3, WORK)), dma((2,)), dma((2,)), dma((2,)), dma((2,)),
                dma((4,)), pltpu.SemaphoreType.REGULAR,
            ],
            compiler_params=pltpu.CompilerParams(
                collective_id=0, has_side_effects=True, vmem_limit_bytes=(64 << 20) - (1 << 19)
            ),
        )(block_list, coupling, left_edge, shard, right_env[0], start)
        return env[None], jnp.swapaxes(state, 1, 2)[None], energy.reshape(1)

    in_specs = (
        P("term", None, None, None),
        P("site", None, None, None, "term"),
        P("site", None, None),
        P("term", "site", None),
        P("site", "term", None, None, None),
        P("site", None, None, "term"),
    )
    out_specs = (P("site", "term", None, None, None), P("site", None, None, "term"), P("site"))
    return jax.shard_map(body, mesh=mesh, in_specs=in_specs, out_specs=out_specs, check_vma=False)
```

```python
import functools

import jax
import jax.numpy as jnp
from jax import lax
from jax.experimental import pallas as pl
from jax.experimental.pallas import tpu as pltpu
from jax.sharding import PartitionSpec as P

ITERS = 4
STEP = 0.5
EPSILON = 1e-06
N = 128
ORB = 4
PHYS = 4
SEC = 2
WORK = 4
PLANES = 4
GROUPS = ((0, 3, 0, 4), (3, 3, 3, 7), (6, 4, 4, 8), (10, 6, 6, 10))
DEEP = max(group[1] for group in GROUPS)
SIDE = 4
MESH = pl.DeviceIdType.MESH
F32, BF16 = jnp.float32, jnp.bfloat16


def split(x):
    high = x.astype(BF16)
    return high, (x - high.astype(F32)).astype(BF16)


def dot(a, b):
    return lax.dot_general(a, b, (((1,), (0,)), ((), ())), preferred_element_type=F32)


def by_plane(plane, field):
    value = jnp.int32(GROUPS[0][field])
    for index, group in enumerate(GROUPS):
        value = jnp.where(plane >= index * PLANES, group[field], value)
    return value


def first_plane(segment):
    value = jnp.int32(0)
    for index, group in enumerate(GROUPS):
        value = jnp.where(segment >= group[0], index * PLANES, value)
    return value


def greetings(sites):
    carrier = {}
    for index, (first, depth, _, _) in enumerate(GROUPS):
        for segment in range(first, first + depth):
            carrier[segment] = index * PLANES
    early, late = set(), set()
    for segment, base in carrier.items():
        early |= {(segment, base + r) for r in range(PLANES)}
        for r in range(PLANES):
            late.add((base + r, segment))
            if segment + 1 < sites:
                late |= {(base + r, carrier[segment + 1] + r), (base + r, segment + 1)}
    early = {(a, b) for a, b in early if a != b}
    late = {(a, b) for a, b in late if a != b and (a, b) not in early}
    return {(b, a) for a, b in early} | late, {(b, a) for a, b in late}


def lookup(site, values):
    chosen = jnp.int32(0)
    for plane, value in enumerate(values):
        chosen = jnp.where(site == plane, value, chosen)
    return chosen


def kernel(
    sites,
    terms,
    perm_ref,
    coup_ref,
    left_ref,
    mps_ref,
    right_ref,
    start_ref,
    env_ref,
    state_ref,
    energy_ref,
    left_in,
    mps_in,
    right_in,
    start_in,
    mine,
    theirs,
    slab,
    slabs,
    coef,
    lanes,
    coefs,
    full,
    starts,
    weights_b,
    scales,
    weights_t,
    enter_hl,
    right_hl,
    cur,
    tx,
    rx,
    vec,
    part,
    pieces,
    reduced,
    gathered,
    quotient,
    pair_ss,
    pair_rs,
    slab_ss,
    slab_rs,
    coef_ss,
    coef_rs,
    leg_ss,
    leg_rs,
    orb_ss,
    orb_rs,
    fwd_ss,
    fwd_rs,
    vec_ss,
    vec_rs,
    tx_sem,
    rx_sem,
    red_ss,
    red_rs,
    gat_ss,
    gat_rs,
    load_sem,
    answered,
):
    site = lax.axis_index("site")
    me = lax.axis_index("term")
    chip, core = me // 2, me % 2
    chips = terms // 2
    sibling = chip * 2 + (1 - core)
    last = sites - 1
    first, depth, ready, steps = (by_plane(site, field) for field in range(4))
    term = lax.rem(site, PLANES)
    x, y = chip % SIDE, chip // SIDE

    loads = [
        pltpu.make_async_copy(outside, inside, load_sem.at[index])
        for index, (outside, inside) in enumerate(
            ((mps_ref, mps_in), (start_ref, start_in), (left_ref, left_in), (right_ref, right_in))
        )
    ]
    for load in loads:
        load.start()

    def along_x(d):
        return {"term": (y * SIDE + lax.rem(x + d, SIDE)) * 2 + core}

    def along_y(d):
        return {"term": (lax.rem(y + d, SIDE) * SIDE + x) * 2 + core}

    barrier = pltpu.get_barrier_semaphore()
    for d in range(1, SIDE):
        for line in (along_x, along_y):
            pl.semaphore_signal(barrier, inc=1, device_id=line(d), device_id_type=MESH)
    pl.semaphore_signal(barrier, inc=1, device_id={"term": sibling}, device_id_type=MESH)
    entry, answers = greetings(sites)

    def signal_planes(pairs, semaphore):
        mask = lookup(site, [sum(1 << b for a, b in pairs if a == plane) for plane in range(sites)])

        def one(other, carry):
            @pl.when((mask >> other) % 2 == 1)
            def _():
                pl.semaphore_signal(semaphore, inc=1, device_id={"site": other}, device_id_type=MESH)

            return carry

        lax.fori_loop(0, sites, one, 0)

    def greeted(pairs):
        return lookup(site, [sum(1 for a, b in pairs if b == plane) for plane in range(sites)])

    signal_planes(entry, barrier)

    loads[0].wait()
    loads[1].wait()
    shard = mps_in[...]
    shard = jnp.concatenate([shard, shard], axis=1).reshape(ORB, 2, 4, 8, N)
    for h in range(2):
        mine[h * 16 : (h + 1) * 16] = shard[:, h].reshape(16, 8, N)
    own = start_in[...]
    mine[32 : 32 + SEC] = jnp.concatenate([own, own], axis=1)

    lane = lax.broadcasted_iota(jnp.int32, (8, N), 1)

    compact = jnp.zeros((8, N), F32)
    for w in range(WORK):
        for o in range(ORB):
            for p in range(PHYS):
                compact = jnp.where(lane == (w * ORB + o) * PHYS + p, coup_ref[w, o, p], compact)
    for o in range(ORB):
        for p in range(PHYS):
            for t in range(SEC):
                index = WORK * ORB * PHYS + (o * PHYS + p) * SEC + t
                compact = jnp.where(lane == index, perm_ref[o, p, t].astype(F32), compact)
    coef[...] = compact
    pl.semaphore_wait(barrier, 2 * (SIDE - 1) + 1 + greeted(entry))
    signal_planes(answers, answered)

    pair = pltpu.make_async_remote_copy(
        src_ref=mine, dst_ref=theirs, send_sem=pair_ss, recv_sem=pair_rs,
        device_id={"term": sibling}, device_id_type=MESH,
    )
    pair.start()
    pair.wait()
    half = lax.broadcasted_iota(jnp.int32, (32 + SEC, 8, N), 1) // 4
    slab[...] = jnp.where(half == core, mine[...], theirs[...])

    source = slab.at[pl.ds(core * 16, 16)]
    to_base = first_plane(site)

    place_of = site - by_plane(to_base, 0)

    def slab_copies(r):
        return [
            pltpu.make_async_remote_copy(
                src_ref=src, dst_ref=dst, send_sem=ss.at[r], recv_sem=rs.at[place_of],
                device_id={"site": to_base + r}, device_id_type=MESH,
            )
            for src, dst, ss, rs in (
                (source, slabs.at[place_of], slab_ss, slab_rs),
                (coef, lanes.at[place_of], coef_ss, coef_rs),
            )
        ]

    def slab_send(r, carry):
        @pl.when(to_base + r == site)
        def _():
            pltpu.make_async_copy(source, slabs.at[place_of], slab_rs.at[place_of]).start()
            pltpu.make_async_copy(coef, lanes.at[place_of], coef_rs.at[place_of]).start()

        @pl.when(to_base + r != site)
        def _():
            for copy in slab_copies(r):
                copy.start()

        return carry

    lax.fori_loop(0, PLANES, slab_send, 0)

    def tiles_of(o):
        return pl.ds(o * 4, 4)

    def row_of(q, o, r):
        return full.at[q, r, :, core, tiles_of(o)]

    def column_of(q, o, c):
        return full.at[q, :, c, core, tiles_of(o)]

    def first_leg(q, o):
        place = full.at[q, y, x, core, tiles_of(o)]
        tiles = slabs.at[q, tiles_of(o)]
        pltpu.make_async_copy(tiles, place, leg_rs.at[q, o]).start()
        for d in range(1, SIDE):
            pltpu.make_async_remote_copy(
                src_ref=tiles, dst_ref=place, send_sem=leg_ss.at[q], recv_sem=leg_rs.at[q, o],
                device_id=(along_x, along_y)[o % 2](d), device_id_type=MESH,
            ).start()

    def second_leg(q, o):
        line = row_of(q, o, y) if o % 2 == 0 else column_of(q, o, x)
        pltpu.make_async_copy(line, line, leg_rs.at[q, o]).wait()
        for d in range(1, SIDE):
            pltpu.make_async_remote_copy(
                src_ref=line, dst_ref=line, send_sem=orb_ss.at[q], recv_sem=orb_rs.at[q, o, d - 1],
                device_id=(along_y, along_x)[o % 2](d), device_id_type=MESH,
            ).start()

    def arrived(q, o, parity):
        for d in range(1, SIDE):
            if parity == 0:
                line = row_of(q, o, lax.rem(y + SIDE - d, SIDE))
            else:
                line = column_of(q, o, lax.rem(x + SIDE - d, SIDE))
            pltpu.make_async_copy(line, line, orb_rs.at[q, o, d - 1]).wait()

    def forward(q, o):
        tiles = full.at[q, :, :, core, tiles_of(o)]
        return pltpu.make_async_remote_copy(
            src_ref=tiles, dst_ref=tiles, send_sem=fwd_ss.at[q, o], recv_sem=fwd_rs.at[q, o],
            device_id={"term": sibling}, device_id_type=MESH,
        )

    row = lax.broadcasted_iota(jnp.int32, (N, N), 0)
    column = lax.broadcasted_iota(jnp.int32, (N, N), 1)

    def turn(i):
        return lax.rem(i + (site - term - first), depth)

    def gather_step(i):
        @pl.when(i < depth)
        def _():
            q = turn(i)
            pltpu.make_async_copy(slabs.at[q], slabs.at[q], slab_rs.at[q]).wait()
            pltpu.make_async_copy(lanes.at[q], lanes.at[q], coef_rs.at[q]).wait()
            for o in range(ORB):
                first_leg(q, o)
            rows = jnp.broadcast_to(lanes[q, 0:1], (N, N)).T
            coefs[q] = jnp.where(row < WORK * ORB * PHYS, jnp.sqrt(rows), rows)

        @pl.when(jnp.logical_and(i >= 1, i < depth + 1))
        def _():
            for o in range(ORB):
                second_leg(turn(i - 1), o)

        @pl.when(jnp.logical_and(i >= 3, i < depth + 3))
        def _():
            for o in range(ORB):
                arrived(turn(i - 3), o, o % 2)
                forward(turn(i - 3), o).start()

    vec_source = slab.at[pl.ds(32, SEC)]

    def side_work():
        pltpu.make_async_copy(vec_source, starts.at[chip], vec_rs).start()

        def vec_copy(d, c):
            peer = lax.rem(chip + d, chips) * 2 + core
            pltpu.make_async_remote_copy(
                src_ref=vec_source, dst_ref=starts.at[chip], send_sem=vec_ss, recv_sem=vec_rs,
                device_id={"term": peer}, device_id_type=MESH,
            ).start()
            return c

        lax.fori_loop(1, chips, vec_copy, 0)

        loads[3].wait()

        def prepare_right(w, carry):
            for s in range(SEC):
                high, low = split(right_in[w, s])
                right_hl[s, pl.ds(w * N, N), 0:N] = high
                right_hl[s, pl.ds(w * N, N), N : 2 * N] = low
            return carry

        lax.fori_loop(0, WORK, prepare_right, 0)


    def coefficient(q, index):
        return coefs[q, pl.ds(index, 1)]

    def sector(q, o, p, t):
        return coefficient(q, WORK * ORB * PHYS + (o * PHYS + p) * SEC + t)

    def prepare(q, o):
        there = full.at[q, :, :, 1 - core, tiles_of(o)]
        pltpu.make_async_copy(there, there, fwd_rs.at[q, o]).wait()
        for p in range(PHYS):
            root = coefficient(q, (term * ORB + o) * PHYS + p)
            columns = slice(p * N, (p + 1) * N)
            rounded, scale = [], []
            for t in range(SEC):
                block = (full[q, :, :, p // 2, o * 4 + (p % 2) * SEC + t].reshape(N, N) * root).T
                size = jnp.maximum(jnp.max(jnp.abs(block), axis=0, keepdims=True) * (128.0 / 255.0), 1e-30)
                near = (block * (1.0 / size)).astype(BF16).astype(F32)
                high, low = split((block - (near * size) * 0.5).T)
                weights_t[q, o, t, 0, :, columns] = high
                weights_t[q, o, t, 1, :, columns] = low
                rounded.append(near)
                scale.append(size)
            source_of_first = sector(q, o, p, 0)
            for s in range(SEC):
                weights_b[q, o, s, :, columns] = jnp.where(source_of_first == s, rounded[0], rounded[1]).astype(BF16)
                scales[q, o, s, 0:1, columns] = jnp.where(source_of_first == s, scale[0], scale[1])

    def orbital(q, o):
        sides = [jnp.concatenate(split(cur[s]), axis=1) for s in range(SEC)]
        pairs = [slice(g * 2 * N, (g + 1) * 2 * N) for g in range(PHYS // 2)]
        moved = []
        for pair_columns in pairs:
            blocks = [weights_b[q, o, s, :, pair_columns] for s in range(SEC)]
            moved.append(
                [
                    dot(sides[s], jnp.concatenate([blocks[s], blocks[s]], axis=0)) * scales[q, o, s, 0:1, pair_columns]
                    for s in range(SEC)
                ]
            )
        totals = [None] * SEC
        for g, pair_columns in enumerate(pairs):
            for t in range(SEC):
                highs, lows = [], []
                for within in range(2):
                    columns = slice(within * N, (within + 1) * N)
                    chosen = sector(q, o, g * 2 + within, t) == 0
                    high, low = split(jnp.where(chosen, moved[g][0][:, columns], moved[g][1][:, columns]))
                    highs.append(high)
                    lows.append(low)
                high, low = jnp.concatenate(highs, axis=0), jnp.concatenate(lows, axis=0)
                wide = dot(weights_t[q, o, t, 0, :, pair_columns], jnp.concatenate([high, low], axis=1))
                y = wide[:, :N] + wide[:, N:] + dot(weights_t[q, o, t, 1, :, pair_columns], high)
                totals[t] = y if g == 0 else totals[t] + y
        for t in range(SEC):
            cur[t] = totals[t] + totals[t].T

    def unpack(kind, w):
        packed = rx[kind, w, 0:N]
        flipped = packed.T
        diagonal = rx[kind, w, N : N + 1]
        return (
            jnp.where(row <= column, packed, flipped),
            jnp.where(row > column, packed, jnp.where(row < column, flipped, diagonal)),
        )

    def message(kind, w, slot, plane):
        return pltpu.make_async_remote_copy(
            src_ref=tx.at[slot], dst_ref=rx.at[kind, w], send_sem=tx_sem.at[kind, slot], recv_sem=rx_sem.at[kind, w],
            device_id={"site": plane}, device_id_type=MESH,
        )

    def received(kind, w):
        pltpu.make_async_copy(rx.at[kind, w], rx.at[kind, w], rx_sem.at[kind, w]).wait()

    def act(copy, start):
        if start:
            copy.start()
        else:
            copy.wait_send()

    def messages(q, start):
        segment = first + q
        after = lax.rem(segment + 1, sites)
        goes_on = jnp.logical_and(q == depth - 1, segment < last)
        pl.when(goes_on)(lambda: act(message(0, term, q, first_plane(after) + term), start))
        pl.when(jnp.logical_and(segment < last, after != site))(lambda: act(message(1, term, q, after), start))
        if start:

            @pl.when(jnp.logical_and(segment < last, after == site))
            def _():
                pltpu.make_async_copy(tx.at[q], rx.at[1, term], rx_sem.at[1, term]).start()

    def results(q, start):
        pl.when(first + q != site)(lambda: act(message(2, term, q, first + q), start))

    def gather_loop(i, carry):
        gather_step(i)

        @pl.when(jnp.logical_and(ready > 0, i >= 4))
        def _():
            for o in range(ORB):
                prepare(turn(i - 4), o)

        pl.when(jnp.logical_and(ready > 0, i == 2))(side_work)
        return carry

    lax.fori_loop(0, steps, gather_loop, 0)
    loads[2].wait()
    pl.semaphore_wait(answered, greeted(answers))

    @pl.when(first == 0)
    def _():
        cur[...] = left_in[term]

    @pl.when(first > 0)
    def _():
        received(0, term)
        cur[0], cur[1] = unpack(0, term)

    def one_segment(q, c):
        pl.when(q + 3 >= steps)(lambda: gather_step(q + 3))

        def inline(o, cc):
            prepare(q, o)
            return cc

        lax.fori_loop(0, jnp.where(q >= ready, ORB, 0), inline, 0)
        for o in range(ORB):
            orbital(q, o)
        tx[q, 0:N] = jnp.where(row <= column, cur[0], cur[1])
        diagonal = jnp.sum(jnp.where(row == column, cur[1], 0.0), axis=0, keepdims=True)
        tx[q, N : N + 8] = jnp.broadcast_to(diagonal, (8, N))
        messages(q, True)

        @pl.when(first + q == site)
        def _():
            env_ref[term] = cur[...]

        return c

    lax.fori_loop(0, depth, one_segment, 0)

    def results_start(q, carry):
        results(q, True)
        return carry

    lax.fori_loop(0, depth, results_start, 0)
    pl.when(ready == 0)(side_work)

    def entering(w, carry):
        pl.when(site > 0)(lambda: received(1, w))

        def keep(blocks):
            for s in range(SEC):
                high, low = split(blocks[s])
                enter_hl[s, pl.ds(w * N, N), 0:N] = high
                enter_hl[s, pl.ds(w * N, N), N : 2 * N] = low

        pl.when(site == 0)(lambda: keep((left_in[w, 0], left_in[w, 1])))
        pl.when(site > 0)(lambda: keep(unpack(1, w)))
        return carry

    lax.fori_loop(0, WORK, entering, 0)

    entries = SEC * N * N
    pltpu.make_async_copy(starts, starts, vec_rs).wait()
    u = [starts[:, s].reshape(N, N) for s in range(SEC)]
    scale = jnp.sqrt((jnp.sum(u[0] * u[0]) + jnp.sum(u[1] * u[1])) / entries + EPSILON)
    for s in range(SEC):
        vec[s] = u[s] / scale

    def total_of(values):
        return jnp.sum(values, axis=(0, 1, 2), keepdims=True)

    offsets = sorted(
        ((a, b, c) for a in range(SIDE) for b in range(SIDE) for c in range(2) if (a, b, c) != (0, 0, 0)),
        key=lambda abc: -min(abc[0], SIDE - abc[0]) - min(abc[1], SIDE - abc[1]),
    )
    far_first = [
        (lax.rem(y + a, SIDE) * SIDE + lax.rem(x + b, SIDE)) * 2 + (core if c == 0 else 1 - core) for a, b, c in offsets
    ]

    def owners_in(rows):
        return [
            (r * SIDE + lax.rem(x + b, SIDE)) * 2 + c
            for r in rows
            for b in (2, 1, 3, 0)
            for c in (core, 1 - core)
        ]

    beside = y + 1 - 2 * (y % 2)
    across = [lax.rem(y + 2, SIDE), lax.rem(beside + 2, SIDE)]
    near_sector = y // 2
    itself = 2 * SIDE + 6
    own_half = owners_in([beside, y])
    halves = ((1 - near_sector, owners_in(across)), (near_sector, own_half[:itself] + own_half[itself + 1 :]))

    def iteration(it, carry):
        slot = lax.rem(it, 2)
        for s, owners in halves:
            high, low = split(vec[s])
            sides = jnp.concatenate(
                [jnp.concatenate([high, low], axis=1), jnp.concatenate([high, jnp.zeros_like(high)], axis=1)], axis=0
            )
            wide = dot(right_hl[s], sides)
            product = wide[:, :N] + wide[:, N:]
            high, low = split(product)
            high = jnp.concatenate([high[w * N : (w + 1) * N] for w in range(WORK)], axis=1)
            low = jnp.concatenate([low[w * N : (w + 1) * N] for w in range(WORK)], axis=1)
            wide = dot(high, enter_hl[s])
            total = wide[:, :N] + wide[:, N:] + dot(low, enter_hl[s, :, 0:N])
            part[slot, pl.ds(s * (N // 8), N // 8)] = total.reshape(N // 8, 8, N)

            for peer in owners:
                pltpu.make_async_remote_copy(
                    src_ref=part.at[slot, peer], dst_ref=pieces.at[slot, me], send_sem=red_ss.at[slot],
                    recv_sem=red_rs.at[slot], device_id={"term": peer}, device_id_type=MESH,
                ).start()

        pltpu.make_async_copy(part.at[slot, me], pieces.at[slot, me], red_rs.at[slot]).start()
        old = vec[...]
        square = total_of(old * old)

        pltpu.make_async_copy(pieces.at[slot], pieces.at[slot], red_rs.at[slot]).wait()
        reduced[slot] = jnp.sum(pieces[slot], axis=0) * (1.0 / (WORK * terms))
        pltpu.make_async_copy(reduced.at[slot], gathered.at[slot, me], gat_rs.at[slot]).start()

        for peer in far_first:
            pltpu.make_async_remote_copy(
                src_ref=reduced.at[slot], dst_ref=gathered.at[slot, me], send_sem=gat_ss.at[slot],
                recv_sem=gat_rs.at[slot], device_id={"term": peer}, device_id_type=MESH,
            ).start()

        pltpu.make_async_copy(gathered.at[slot], gathered.at[slot], gat_rs.at[slot]).wait()
        sent = pieces.at[slot, pl.ds(0, terms - 1)]
        pltpu.make_async_copy(sent, sent, red_ss.at[slot]).wait()
        pltpu.make_async_copy(sent, sent, gat_ss.at[slot]).wait()

        image = gathered[slot].reshape(SEC, N, N)
        rayleigh = total_of(old * image) / square
        corrected = old - STEP * (image - rayleigh * old)
        vec[...] = corrected / jnp.sqrt(total_of(corrected * corrected) / entries + EPSILON)
        quotient[...] = jnp.broadcast_to(rayleigh[0], (8, N))
        return carry

    lax.fori_loop(0, ITERS, iteration, 0)
    energy_ref[0, 0] = quotient[0, 0]
    for s in range(SEC):
        rows = vec[s, pl.ds(pl.multiple_of(chip * 8, 8), 8)]
        state_ref[s] = jnp.where(core == 0, rows[0:4], rows[4:8])

    def leaving(w, carry):
        @pl.when(first_plane(site) + w != site)
        def _():
            received(2, w)
            env_ref[w, 0], env_ref[w, 1] = unpack(2, w)

        return carry

    lax.fori_loop(0, WORK, leaving, 0)

    def slab_done(r, carry):
        @pl.when(to_base + r != site)
        def _():
            for copy in slab_copies(r):
                copy.wait_send()

        return carry

    lax.fori_loop(0, PLANES, slab_done, 0)

    def spread_done(q, carry):
        sent = full.at[q, 0, pl.ds(0, SIDE - 1), 0]
        pltpu.make_async_copy(sent, sent, leg_ss.at[q]).wait()
        sent = full.at[q, pl.ds(0, SIDE - 1), :, 0]
        pltpu.make_async_copy(sent, sent, orb_ss.at[q]).wait()
        for o in range(ORB):
            forward(q, o).wait_send()
        return carry

    lax.fori_loop(0, depth, spread_done, 0)
    vec_sent = starts.at[pl.ds(0, chips - 1)]
    pltpu.make_async_copy(vec_sent, vec_sent, vec_ss).wait()

    def messages_done(q, carry):
        messages(q, False)
        results(q, False)
        return carry

    lax.fori_loop(0, depth, messages_done, 0)


def solution(mesh):
    sites, terms = mesh.shape["site"], mesh.shape["term"]
    chips = terms // 2

    def body(left_edge, mps, block_list, coupling, right_env, start_vector):
        shard = jnp.swapaxes(mps, 3, 4).reshape(ORB * 8, 4, N)
        start = jnp.swapaxes(start_vector[0], 1, 2)
        vmem = pl.BlockSpec(memory_space=pltpu.VMEM)
        anywhere = pl.BlockSpec(memory_space=pltpu.HBM)
        smem = pl.BlockSpec(memory_space=pltpu.SMEM)
        dma = pltpu.SemaphoreType.DMA
        env, state, energy = pl.pallas_call(
            functools.partial(kernel, sites, terms),
            out_shape=(
                jax.ShapeDtypeStruct((WORK, SEC, N, N), F32),
                jax.ShapeDtypeStruct((SEC, 4, N), F32),
                jax.ShapeDtypeStruct((1, 1), F32),
            ),
            in_specs=[smem, smem, anywhere, anywhere, anywhere, anywhere],
            out_specs=(vmem, vmem, smem),
            scratch_shapes=[
                pltpu.VMEM((WORK, SEC, N, N), F32),
                pltpu.VMEM((ORB * 8, 4, N), F32),
                pltpu.VMEM((WORK, SEC, N, N), F32),
                pltpu.VMEM((SEC, 4, N), F32),
                pltpu.VMEM((32 + SEC, 8, N), F32),
                pltpu.VMEM((32 + SEC, 8, N), F32),
                pltpu.VMEM((32 + SEC, 8, N), F32),
                pltpu.VMEM((DEEP, 16, 8, N), F32),
                pltpu.VMEM((8, N), F32),
                pltpu.VMEM((DEEP, 8, N), F32),
                pltpu.VMEM((DEEP, N, N), F32),
                pltpu.VMEM((DEEP, SIDE, SIDE, 2, 16, 8, N), F32),
                pltpu.VMEM((chips, SEC, 8, N), F32),
                pltpu.VMEM((DEEP, ORB, SEC, N, PHYS * N), BF16),
                pltpu.VMEM((DEEP, ORB, SEC, 8, PHYS * N), F32),
                pltpu.VMEM((DEEP, ORB, SEC, 2, N, PHYS * N), BF16),
                pltpu.VMEM((SEC, WORK * N, 2 * N), BF16),
                pltpu.VMEM((SEC, WORK * N, 2 * N), BF16),
                pltpu.VMEM((SEC, N, N), F32),
                pltpu.VMEM((DEEP, N + 8, N), F32),
                pltpu.VMEM((3, WORK, N + 8, N), F32),
                pltpu.VMEM((SEC, N, N), F32),
                pltpu.VMEM((2, terms, 8, N), F32),
                pltpu.VMEM((2, terms, 8, N), F32),
                pltpu.VMEM((2, 8, N), F32),
                pltpu.VMEM((2, terms, 8, N), F32),
                pltpu.VMEM((8, N), F32),
                dma, dma, dma((PLANES,)), dma((DEEP,)), dma((PLANES,)), dma((DEEP,)),
                dma((DEEP,)), dma((DEEP, ORB)), dma((DEEP,)), dma((DEEP, ORB, SIDE - 1)), dma((DEEP, ORB)), dma((DEEP, ORB)),
                dma, dma, dma((3, DEEP)), dma((3, WORK)), dma((2,)), dma((2,)), dma((2,)), dma((2,)),
                dma((4,)), pltpu.SemaphoreType.REGULAR,
            ],
            compiler_params=pltpu.CompilerParams(
                collective_id=0, has_side_effects=True, vmem_limit_bytes=(64 << 20) - (1 << 19)
            ),
        )(block_list, coupling, left_edge, shard, right_env[0], start)
        return env[None], jnp.swapaxes(state, 1, 2)[None], energy.reshape(1)

    in_specs = (
        P("term", None, None, None),
        P("site", None, None, None, "term"),
        P("site", None, None),
        P("term", "site", None),
        P("site", "term", None, None, None),
        P("site", None, None, "term"),
    )
    out_specs = (P("site", "term", None, None, None), P("site", None, None, "term"), P("site"))
    return jax.shard_map(body, mesh=mesh, in_specs=in_specs, out_specs=out_specs, check_vma=False)
```

```python
import functools

import jax
import jax.numpy as jnp
from jax import lax
from jax.experimental import pallas as pl
from jax.experimental.pallas import tpu as pltpu
from jax.sharding import PartitionSpec as P

ITERS = 4
STEP = 0.5
EPSILON = 1e-06
N = 128
ORB = 4
PHYS = 4
SEC = 2
WORK = 4
PLANES = 4
GROUPS = ((0, 3, 0, 4), (3, 3, 3, 7), (6, 4, 4, 8), (10, 6, 6, 10))
DEEP = max(group[1] for group in GROUPS)
SIDE = 4
MESH = pl.DeviceIdType.MESH
F32, BF16 = jnp.float32, jnp.bfloat16


def split(x):
    high = x.astype(BF16)
    return high, (x - high.astype(F32)).astype(BF16)


def dot(a, b):
    return lax.dot_general(a, b, (((1,), (0,)), ((), ())), preferred_element_type=F32)


def by_plane(plane, field):
    value = jnp.int32(GROUPS[0][field])
    for index, group in enumerate(GROUPS):
        value = jnp.where(plane >= index * PLANES, group[field], value)
    return value


def first_plane(segment):
    value = jnp.int32(0)
    for index, group in enumerate(GROUPS):
        value = jnp.where(segment >= group[0], index * PLANES, value)
    return value


def greetings(sites):
    carrier = {}
    for index, (first, depth, _, _) in enumerate(GROUPS):
        for segment in range(first, first + depth):
            carrier[segment] = index * PLANES
    early, late = set(), set()
    for segment, base in carrier.items():
        early |= {(segment, base + r) for r in range(PLANES)}
        for r in range(PLANES):
            late.add((base + r, segment))
            if segment + 1 < sites:
                late |= {(base + r, carrier[segment + 1] + r), (base + r, segment + 1)}
    early = {(a, b) for a, b in early if a != b}
    late = {(a, b) for a, b in late if a != b and (a, b) not in early}
    return {(b, a) for a, b in early} | late, {(b, a) for a, b in late}


def lookup(site, values):
    chosen = jnp.int32(0)
    for plane, value in enumerate(values):
        chosen = jnp.where(site == plane, value, chosen)
    return chosen


def kernel(
    sites,
    terms,
    perm_ref,
    coup_ref,
    left_ref,
    mps_ref,
    right_ref,
    start_ref,
    env_ref,
    state_ref,
    energy_ref,
    left_in,
    mps_in,
    right_in,
    start_in,
    mine,
    theirs,
    slab,
    slabs,
    coef,
    lanes,
    coefs,
    full,
    starts,
    weights_b,
    scales,
    weights_t,
    enter_hl,
    right_hl,
    cur,
    tx,
    rx,
    vec,
    part,
    pieces,
    reduced,
    gathered,
    quotient,
    pair_ss,
    pair_rs,
    slab_ss,
    slab_rs,
    coef_ss,
    coef_rs,
    leg_ss,
    leg_rs,
    orb_ss,
    orb_rs,
    fwd_ss,
    fwd_rs,
    vec_ss,
    vec_rs,
    tx_sem,
    rx_sem,
    red_ss,
    red_rs,
    gat_ss,
    gat_rs,
    load_sem,
    answered,
):
    site = lax.axis_index("site")
    me = lax.axis_index("term")
    chip, core = me // 2, me % 2
    chips = terms // 2
    sibling = chip * 2 + (1 - core)
    last = sites - 1
    first, depth, ready, steps = (by_plane(site, field) for field in range(4))
    term = lax.rem(site, PLANES)
    x, y = chip % SIDE, chip // SIDE

    loads = [
        pltpu.make_async_copy(outside, inside, load_sem.at[index])
        for index, (outside, inside) in enumerate(
            ((mps_ref, mps_in), (start_ref, start_in), (left_ref, left_in), (right_ref, right_in))
        )
    ]
    for load in loads:
        load.start()

    def along_x(d):
        return {"term": (y * SIDE + lax.rem(x + d, SIDE)) * 2 + core}

    def along_y(d):
        return {"term": (lax.rem(y + d, SIDE) * SIDE + x) * 2 + core}

    barrier = pltpu.get_barrier_semaphore()
    for d in range(1, SIDE):
        for line in (along_x, along_y):
            pl.semaphore_signal(barrier, inc=1, device_id=line(d), device_id_type=MESH)
    pl.semaphore_signal(barrier, inc=1, device_id={"term": sibling}, device_id_type=MESH)
    entry, answers = greetings(sites)

    def signal_planes(pairs, semaphore):
        mask = lookup(site, [sum(1 << b for a, b in pairs if a == plane) for plane in range(sites)])

        def one(other, carry):
            @pl.when((mask >> other) % 2 == 1)
            def _():
                pl.semaphore_signal(semaphore, inc=1, device_id={"site": other}, device_id_type=MESH)

            return carry

        lax.fori_loop(0, sites, one, 0)

    def greeted(pairs):
        return lookup(site, [sum(1 for a, b in pairs if b == plane) for plane in range(sites)])

    signal_planes(entry, barrier)

    loads[0].wait()
    loads[1].wait()
    shard = mps_in[...]
    shard = jnp.concatenate([shard, shard], axis=1).reshape(ORB, 2, 4, 8, N)
    for h in range(2):
        mine[h * 16 : (h + 1) * 16] = shard[:, h].reshape(16, 8, N)
    own = start_in[...]
    mine[32 : 32 + SEC] = jnp.concatenate([own, own], axis=1)

    lane = lax.broadcasted_iota(jnp.int32, (8, N), 1)

    compact = jnp.zeros((8, N), F32)
    for w in range(WORK):
        for o in range(ORB):
            for p in range(PHYS):
                compact = jnp.where(lane == (w * ORB + o) * PHYS + p, coup_ref[w, o, p], compact)
    for o in range(ORB):
        for p in range(PHYS):
            for t in range(SEC):
                index = WORK * ORB * PHYS + (o * PHYS + p) * SEC + t
                compact = jnp.where(lane == index, perm_ref[o, p, t].astype(F32), compact)
    coef[...] = compact
    pl.semaphore_wait(barrier, 2 * (SIDE - 1) + 1 + greeted(entry))
    signal_planes(answers, answered)

    pair = pltpu.make_async_remote_copy(
        src_ref=mine, dst_ref=theirs, send_sem=pair_ss, recv_sem=pair_rs,
        device_id={"term": sibling}, device_id_type=MESH,
    )
    pair.start()
    pair.wait()
    half = lax.broadcasted_iota(jnp.int32, (32 + SEC, 8, N), 1) // 4
    slab[...] = jnp.where(half == core, mine[...], theirs[...])

    source = slab.at[pl.ds(core * 16, 16)]
    to_base = first_plane(site)

    place_of = site - by_plane(to_base, 0)

    def slab_copies(r):
        return [
            pltpu.make_async_remote_copy(
                src_ref=src, dst_ref=dst, send_sem=ss.at[r], recv_sem=rs.at[place_of],
                device_id={"site": to_base + r}, device_id_type=MESH,
            )
            for src, dst, ss, rs in (
                (source, slabs.at[place_of], slab_ss, slab_rs),
                (coef, lanes.at[place_of], coef_ss, coef_rs),
            )
        ]

    def slab_send(r, carry):
        @pl.when(to_base + r == site)
        def _():
            pltpu.make_async_copy(source, slabs.at[place_of], slab_rs.at[place_of]).start()
            pltpu.make_async_copy(coef, lanes.at[place_of], coef_rs.at[place_of]).start()

        @pl.when(to_base + r != site)
        def _():
            for copy in slab_copies(r):
                copy.start()

        return carry

    lax.fori_loop(0, PLANES, slab_send, 0)

    def tiles_of(o):
        return pl.ds(o * 4, 4)

    def row_of(q, o, r):
        return full.at[q, r, :, core, tiles_of(o)]

    def column_of(q, o, c):
        return full.at[q, :, c, core, tiles_of(o)]

    def first_leg(q, o):
        place = full.at[q, y, x, core, tiles_of(o)]
        tiles = slabs.at[q, tiles_of(o)]
        pltpu.make_async_copy(tiles, place, leg_rs.at[q, o]).start()
        for d in range(1, SIDE):
            pltpu.make_async_remote_copy(
                src_ref=tiles, dst_ref=place, send_sem=leg_ss.at[q], recv_sem=leg_rs.at[q, o],
                device_id=(along_x, along_y)[o % 2](d), device_id_type=MESH,
            ).start()

    def second_leg(q, o):
        line = row_of(q, o, y) if o % 2 == 0 else column_of(q, o, x)
        pltpu.make_async_copy(line, line, leg_rs.at[q, o]).wait()
        for d in range(1, SIDE):
            pltpu.make_async_remote_copy(
                src_ref=line, dst_ref=line, send_sem=orb_ss.at[q], recv_sem=orb_rs.at[q, o, d - 1],
                device_id=(along_y, along_x)[o % 2](d), device_id_type=MESH,
            ).start()

    def arrived(q, o, parity):
        for d in range(1, SIDE):
            if parity == 0:
                line = row_of(q, o, lax.rem(y + SIDE - d, SIDE))
            else:
                line = column_of(q, o, lax.rem(x + SIDE - d, SIDE))
            pltpu.make_async_copy(line, line, orb_rs.at[q, o, d - 1]).wait()

    def forward(q, o):
        tiles = full.at[q, :, :, core, tiles_of(o)]
        return pltpu.make_async_remote_copy(
            src_ref=tiles, dst_ref=tiles, send_sem=fwd_ss.at[q, o], recv_sem=fwd_rs.at[q, o],
            device_id={"term": sibling}, device_id_type=MESH,
        )

    row = lax.broadcasted_iota(jnp.int32, (N, N), 0)
    column = lax.broadcasted_iota(jnp.int32, (N, N), 1)

    def turn(i):
        return lax.rem(i + (site - term - first), depth)

    def gather_step(i):
        @pl.when(i < depth)
        def _():
            q = turn(i)
            pltpu.make_async_copy(slabs.at[q], slabs.at[q], slab_rs.at[q]).wait()
            pltpu.make_async_copy(lanes.at[q], lanes.at[q], coef_rs.at[q]).wait()
            for o in range(ORB):
                first_leg(q, o)
            rows = jnp.broadcast_to(lanes[q, 0:1], (N, N)).T
            coefs[q] = jnp.where(row < WORK * ORB * PHYS, jnp.sqrt(rows), rows)

        @pl.when(jnp.logical_and(i >= 1, i < depth + 1))
        def _():
            for o in range(ORB):
                second_leg(turn(i - 1), o)

        @pl.when(jnp.logical_and(i >= 3, i < depth + 3))
        def _():
            for o in range(ORB):
                arrived(turn(i - 3), o, o % 2)
                forward(turn(i - 3), o).start()

    vec_source = slab.at[pl.ds(32, SEC)]

    def side_work():
        pltpu.make_async_copy(vec_source, starts.at[chip], vec_rs).start()

        def vec_copy(d, c):
            peer = lax.rem(chip + d, chips) * 2 + core
            pltpu.make_async_remote_copy(
                src_ref=vec_source, dst_ref=starts.at[chip], send_sem=vec_ss, recv_sem=vec_rs,
                device_id={"term": peer}, device_id_type=MESH,
            ).start()
            return c

        lax.fori_loop(1, chips, vec_copy, 0)

        loads[3].wait()

        def prepare_right(w, carry):
            for s in range(SEC):
                high, low = split(right_in[w, s])
                right_hl[s, pl.ds(w * N, N), 0:N] = high
                right_hl[s, pl.ds(w * N, N), N : 2 * N] = low
            return carry

        lax.fori_loop(0, WORK, prepare_right, 0)


    def coefficient(q, index):
        return coefs[q, pl.ds(index, 1)]

    def sector(q, o, p, t):
        return coefficient(q, WORK * ORB * PHYS + (o * PHYS + p) * SEC + t)

    def prepare(q, o):
        there = full.at[q, :, :, 1 - core, tiles_of(o)]
        pltpu.make_async_copy(there, there, fwd_rs.at[q, o]).wait()
        for p in range(PHYS):
            root = coefficient(q, (term * ORB + o) * PHYS + p)
            columns = slice(p * N, (p + 1) * N)
            rounded, scale = [], []
            for t in range(SEC):
                block = (full[q, :, :, p // 2, o * 4 + (p % 2) * SEC + t].reshape(N, N) * root).T
                size = jnp.maximum(jnp.max(jnp.abs(block), axis=0, keepdims=True) * (128.0 / 255.0), 1e-30)
                near = (block * (1.0 / size)).astype(BF16).astype(F32)
                high, low = split((block - (near * size) * 0.5).T)
                weights_t[q, o, t, 0, :, columns] = high
                weights_t[q, o, t, 1, :, columns] = low
                rounded.append(near)
                scale.append(size)
            source_of_first = sector(q, o, p, 0)
            for s in range(SEC):
                weights_b[q, o, s, :, columns] = jnp.where(source_of_first == s, rounded[0], rounded[1]).astype(BF16)
                scales[q, o, s, 0:1, columns] = jnp.where(source_of_first == s, scale[0], scale[1])

    def orbital(q, o):
        sides = [jnp.concatenate(split(cur[s]), axis=1) for s in range(SEC)]
        pairs = [slice(g * 2 * N, (g + 1) * 2 * N) for g in range(PHYS // 2)]
        moved = []
        for pair_columns in pairs:
            blocks = [weights_b[q, o, s, :, pair_columns] for s in range(SEC)]
            moved.append(
                [
                    dot(sides[s], jnp.concatenate([blocks[s], blocks[s]], axis=0)) * scales[q, o, s, 0:1, pair_columns]
                    for s in range(SEC)
                ]
            )
        totals = [None] * SEC
        for g, pair_columns in enumerate(pairs):
            for t in range(SEC):
                highs, lows = [], []
                for within in range(2):
                    columns = slice(within * N, (within + 1) * N)
                    chosen = sector(q, o, g * 2 + within, t) == 0
                    high, low = split(jnp.where(chosen, moved[g][0][:, columns], moved[g][1][:, columns]))
                    highs.append(high)
                    lows.append(low)
                high, low = jnp.concatenate(highs, axis=0), jnp.concatenate(lows, axis=0)
                wide = dot(weights_t[q, o, t, 0, :, pair_columns], jnp.concatenate([high, low], axis=1))
                y = wide[:, :N] + wide[:, N:] + dot(weights_t[q, o, t, 1, :, pair_columns], high)
                totals[t] = y if g == 0 else totals[t] + y
        for t in range(SEC):
            cur[t] = totals[t] + totals[t].T

    def unpack(kind, w):
        packed = rx[kind, w, 0:N]
        flipped = packed.T
        diagonal = rx[kind, w, N : N + 1]
        return (
            jnp.where(row <= column, packed, flipped),
            jnp.where(row > column, packed, jnp.where(row < column, flipped, diagonal)),
        )

    def message(kind, w, slot, plane):
        return pltpu.make_async_remote_copy(
            src_ref=tx.at[slot], dst_ref=rx.at[kind, w], send_sem=tx_sem.at[kind, slot], recv_sem=rx_sem.at[kind, w],
            device_id={"site": plane}, device_id_type=MESH,
        )

    def received(kind, w):
        pltpu.make_async_copy(rx.at[kind, w], rx.at[kind, w], rx_sem.at[kind, w]).wait()

    def act(copy, start):
        if start:
            copy.start()
        else:
            copy.wait_send()

    def messages(q, start):
        segment = first + q
        after = lax.rem(segment + 1, sites)
        goes_on = jnp.logical_and(q == depth - 1, segment < last)
        pl.when(goes_on)(lambda: act(message(0, term, q, first_plane(after) + term), start))
        pl.when(jnp.logical_and(segment < last, after != site))(lambda: act(message(1, term, q, after), start))
        if start:

            @pl.when(jnp.logical_and(segment < last, after == site))
            def _():
                pltpu.make_async_copy(tx.at[q], rx.at[1, term], rx_sem.at[1, term]).start()

    def results(q, start):
        pl.when(first + q != site)(lambda: act(message(2, term, q, first + q), start))

    def gather_loop(i, carry):
        gather_step(i)

        @pl.when(jnp.logical_and(ready > 0, i >= 4))
        def _():
            for o in range(ORB):
                prepare(turn(i - 4), o)

        pl.when(jnp.logical_and(ready > 0, i == 2))(side_work)
        return carry

    lax.fori_loop(0, steps, gather_loop, 0)
    loads[2].wait()
    pl.semaphore_wait(answered, greeted(answers))

    @pl.when(first == 0)
    def _():
        cur[...] = left_in[term]

    @pl.when(first > 0)
    def _():
        received(0, term)
        cur[0], cur[1] = unpack(0, term)

    def one_segment(q, c):
        pl.when(q + 3 >= steps)(lambda: gather_step(q + 3))

        def inline(o, cc):
            prepare(q, o)
            return cc

        lax.fori_loop(0, jnp.where(q >= ready, ORB, 0), inline, 0)
        for o in range(ORB):
            orbital(q, o)
        tx[q, 0:N] = jnp.where(row <= column, cur[0], cur[1])
        diagonal = jnp.sum(jnp.where(row == column, cur[1], 0.0), axis=0, keepdims=True)
        tx[q, N : N + 8] = jnp.broadcast_to(diagonal, (8, N))
        messages(q, True)

        @pl.when(first + q == site)
        def _():
            env_ref[term] = cur[...]

        return c

    lax.fori_loop(0, depth, one_segment, 0)

    def results_start(q, carry):
        results(q, True)
        return carry

    lax.fori_loop(0, depth, results_start, 0)
    pl.when(ready == 0)(side_work)

    def entering(w, carry):
        pl.when(site > 0)(lambda: received(1, w))

        def keep(blocks):
            for s in range(SEC):
                high, low = split(blocks[s])
                enter_hl[s, pl.ds(w * N, N), 0:N] = high
                enter_hl[s, pl.ds(w * N, N), N : 2 * N] = low

        pl.when(site == 0)(lambda: keep((left_in[w, 0], left_in[w, 1])))
        pl.when(site > 0)(lambda: keep(unpack(1, w)))
        return carry

    lax.fori_loop(0, WORK, entering, 0)

    entries = SEC * N * N
    pltpu.make_async_copy(starts, starts, vec_rs).wait()
    u = [starts[:, s].reshape(N, N) for s in range(SEC)]
    scale = jnp.sqrt((jnp.sum(u[0] * u[0]) + jnp.sum(u[1] * u[1])) / entries + EPSILON)
    for s in range(SEC):
        vec[s] = u[s] / scale

    def total_of(values):
        return jnp.sum(values, axis=(0, 1, 2), keepdims=True)

    offsets = sorted(
        ((a, b, c) for a in range(SIDE) for b in range(SIDE) for c in range(2) if (a, b, c) != (0, 0, 0)),
        key=lambda abc: -min(abc[0], SIDE - abc[0]) - min(abc[1], SIDE - abc[1]),
    )
    far_first = [
        (lax.rem(y + a, SIDE) * SIDE + lax.rem(x + b, SIDE)) * 2 + (core if c == 0 else 1 - core) for a, b, c in offsets
    ]

    def owners_in(rows):
        return [
            (r * SIDE + lax.rem(x + b, SIDE)) * 2 + c
            for r in rows
            for b in (2, 1, 3, 0)
            for c in (core, 1 - core)
        ]

    beside = y + 1 - 2 * (y % 2)
    across = [lax.rem(y + 2, SIDE), lax.rem(beside + 2, SIDE)]
    near_sector = y // 2
    itself = 2 * SIDE + 6
    own_half = owners_in([beside, y])
    halves = ((1 - near_sector, owners_in(across)), (near_sector, own_half[:itself] + own_half[itself + 1 :]))

    def leaving(w, carry):
        @pl.when(first_plane(site) + w != site)
        def _():
            received(2, w)
            env_ref[w, 0], env_ref[w, 1] = unpack(2, w)

        return carry

    def iteration(it, carry):
        slot = lax.rem(it, 2)
        for s, owners in halves:
            high, low = split(vec[s])
            sides = jnp.concatenate(
                [jnp.concatenate([high, low], axis=1), jnp.concatenate([high, jnp.zeros_like(high)], axis=1)], axis=0
            )
            wide = dot(right_hl[s], sides)
            product = wide[:, :N] + wide[:, N:]
            high, low = split(product)
            high = jnp.concatenate([high[w * N : (w + 1) * N] for w in range(WORK)], axis=1)
            low = jnp.concatenate([low[w * N : (w + 1) * N] for w in range(WORK)], axis=1)
            wide = dot(high, enter_hl[s])
            total = wide[:, :N] + wide[:, N:] + dot(low, enter_hl[s, :, 0:N])
            part[slot, pl.ds(s * (N // 8), N // 8)] = total.reshape(N // 8, 8, N)

            for peer in owners:
                pltpu.make_async_remote_copy(
                    src_ref=part.at[slot, peer], dst_ref=pieces.at[slot, me], send_sem=red_ss.at[slot],
                    recv_sem=red_rs.at[slot], device_id={"term": peer}, device_id_type=MESH,
                ).start()

        pltpu.make_async_copy(part.at[slot, me], pieces.at[slot, me], red_rs.at[slot]).start()
        old = vec[...]
        square = total_of(old * old)
        leaving(lax.rem(it + WORK - 1, WORK), 0)

        pltpu.make_async_copy(pieces.at[slot], pieces.at[slot], red_rs.at[slot]).wait()
        reduced[slot] = jnp.sum(pieces[slot], axis=0) * (1.0 / (WORK * terms))
        pltpu.make_async_copy(reduced.at[slot], gathered.at[slot, me], gat_rs.at[slot]).start()

        for peer in far_first:
            pltpu.make_async_remote_copy(
                src_ref=reduced.at[slot], dst_ref=gathered.at[slot, me], send_sem=gat_ss.at[slot],
                recv_sem=gat_rs.at[slot], device_id={"term": peer}, device_id_type=MESH,
            ).start()

        pltpu.make_async_copy(gathered.at[slot], gathered.at[slot], gat_rs.at[slot]).wait()
        sent = pieces.at[slot, pl.ds(0, terms - 1)]
        pltpu.make_async_copy(sent, sent, red_ss.at[slot]).wait()
        pltpu.make_async_copy(sent, sent, gat_ss.at[slot]).wait()

        image = gathered[slot].reshape(SEC, N, N)
        rayleigh = total_of(old * image) / square
        corrected = old - STEP * (image - rayleigh * old)
        vec[...] = corrected / jnp.sqrt(total_of(corrected * corrected) / entries + EPSILON)
        quotient[...] = jnp.broadcast_to(rayleigh[0], (8, N))
        return carry

    lax.fori_loop(0, ITERS, iteration, 0)
    energy_ref[0, 0] = quotient[0, 0]
    for s in range(SEC):
        rows = vec[s, pl.ds(pl.multiple_of(chip * 8, 8), 8)]
        state_ref[s] = jnp.where(core == 0, rows[0:4], rows[4:8])

    def slab_done(r, carry):
        @pl.when(to_base + r != site)
        def _():
            for copy in slab_copies(r):
                copy.wait_send()

        return carry

    lax.fori_loop(0, PLANES, slab_done, 0)

    def spread_done(q, carry):
        sent = full.at[q, 0, pl.ds(0, SIDE - 1), 0]
        pltpu.make_async_copy(sent, sent, leg_ss.at[q]).wait()
        sent = full.at[q, pl.ds(0, SIDE - 1), :, 0]
        pltpu.make_async_copy(sent, sent, orb_ss.at[q]).wait()
        for o in range(ORB):
            forward(q, o).wait_send()
        return carry

    lax.fori_loop(0, depth, spread_done, 0)
    vec_sent = starts.at[pl.ds(0, chips - 1)]
    pltpu.make_async_copy(vec_sent, vec_sent, vec_ss).wait()

    def messages_done(q, carry):
        messages(q, False)
        results(q, False)
        return carry

    lax.fori_loop(0, depth, messages_done, 0)


def solution(mesh):
    sites, terms = mesh.shape["site"], mesh.shape["term"]
    chips = terms // 2

    def body(left_edge, mps, block_list, coupling, right_env, start_vector):
        shard = jnp.swapaxes(mps, 3, 4).reshape(ORB * 8, 4, N)
        start = jnp.swapaxes(start_vector[0], 1, 2)
        vmem = pl.BlockSpec(memory_space=pltpu.VMEM)
        anywhere = pl.BlockSpec(memory_space=pltpu.HBM)
        smem = pl.BlockSpec(memory_space=pltpu.SMEM)
        dma = pltpu.SemaphoreType.DMA
        env, state, energy = pl.pallas_call(
            functools.partial(kernel, sites, terms),
            out_shape=(
                jax.ShapeDtypeStruct((WORK, SEC, N, N), F32),
                jax.ShapeDtypeStruct((SEC, 4, N), F32),
                jax.ShapeDtypeStruct((1, 1), F32),
            ),
            in_specs=[smem, smem, anywhere, anywhere, anywhere, anywhere],
            out_specs=(vmem, vmem, smem),
            scratch_shapes=[
                pltpu.VMEM((WORK, SEC, N, N), F32),
                pltpu.VMEM((ORB * 8, 4, N), F32),
                pltpu.VMEM((WORK, SEC, N, N), F32),
                pltpu.VMEM((SEC, 4, N), F32),
                pltpu.VMEM((32 + SEC, 8, N), F32),
                pltpu.VMEM((32 + SEC, 8, N), F32),
                pltpu.VMEM((32 + SEC, 8, N), F32),
                pltpu.VMEM((DEEP, 16, 8, N), F32),
                pltpu.VMEM((8, N), F32),
                pltpu.VMEM((DEEP, 8, N), F32),
                pltpu.VMEM((DEEP, N, N), F32),
                pltpu.VMEM((DEEP, SIDE, SIDE, 2, 16, 8, N), F32),
                pltpu.VMEM((chips, SEC, 8, N), F32),
                pltpu.VMEM((DEEP, ORB, SEC, N, PHYS * N), BF16),
                pltpu.VMEM((DEEP, ORB, SEC, 8, PHYS * N), F32),
                pltpu.VMEM((DEEP, ORB, SEC, 2, N, PHYS * N), BF16),
                pltpu.VMEM((SEC, WORK * N, 2 * N), BF16),
                pltpu.VMEM((SEC, WORK * N, 2 * N), BF16),
                pltpu.VMEM((SEC, N, N), F32),
                pltpu.VMEM((DEEP, N + 8, N), F32),
                pltpu.VMEM((3, WORK, N + 8, N), F32),
                pltpu.VMEM((SEC, N, N), F32),
                pltpu.VMEM((2, terms, 8, N), F32),
                pltpu.VMEM((2, terms, 8, N), F32),
                pltpu.VMEM((2, 8, N), F32),
                pltpu.VMEM((2, terms, 8, N), F32),
                pltpu.VMEM((8, N), F32),
                dma, dma, dma((PLANES,)), dma((DEEP,)), dma((PLANES,)), dma((DEEP,)),
                dma((DEEP,)), dma((DEEP, ORB)), dma((DEEP,)), dma((DEEP, ORB, SIDE - 1)), dma((DEEP, ORB)), dma((DEEP, ORB)),
                dma, dma, dma((3, DEEP)), dma((3, WORK)), dma((2,)), dma((2,)), dma((2,)), dma((2,)),
                dma((4,)), pltpu.SemaphoreType.REGULAR,
            ],
            compiler_params=pltpu.CompilerParams(
                collective_id=0, has_side_effects=True, vmem_limit_bytes=(64 << 20) - (1 << 19)
            ),
        )(block_list, coupling, left_edge, shard, right_env[0], start)
        return env[None], jnp.swapaxes(state, 1, 2)[None], energy.reshape(1)

    in_specs = (
        P("term", None, None, None),
        P("site", None, None, None, "term"),
        P("site", None, None),
        P("term", "site", None),
        P("site", "term", None, None, None),
        P("site", None, None, "term"),
    )
    out_specs = (P("site", "term", None, None, None), P("site", None, None, "term"), P("site"))
    return jax.shard_map(body, mesh=mesh, in_specs=in_specs, out_specs=out_specs, check_vma=False)
```
